32 devices in a mesh: seq: 8 (over z, y), head: 4 (over x, core).
Axes of the slice: x: 2, y: 2, z: 4, core: 2. Of those that a mesh axis runs over, the one named last changes fastest.
Arguments:
- queries: bfloat16 [1024, 8, 1024], P('seq', 'head'), may hold values from -6 to 6
- keys: bfloat16 [1024, 1024], P('seq', 'head'), may hold values from -6 to 6
- values: bfloat16 [1024, 1024], P('seq', 'head'), may hold values from -6 to 6
- out_grad: bfloat16 [1024, 8, 1024], P('seq', 'head'), may hold values from -6 to 6
- doc_ids: int32 [1024], P('seq'), may hold values from 0 to 3, never falling along the last dimension, each value on 1 to 384 neighbouring positions
Outputs:
- attended: bfloat16 [1024, 8, 1024], P('seq', 'head')
- query_grad: bfloat16 [1024, 8, 1024], P('seq', 'head')
- key_grad: bfloat16 [1024, 1024], P('seq', 'head')
- value_grad: bfloat16 [1024, 1024], P('seq', 'head')
The draws below stay inside these ranges and needn't reach their ends.
Inputs may be any that keep to these rules, and one draw needn't show every extreme that they name: `doc_ids`: document ids never fall; each document has at most 384 tokens, one exactly that many.
All inputs are finite; a program needn't handle non-finite values.
Results may differ from the reference program's by a relative error of at most 0.0067.
Values may be sent and summed in bfloat16 or wider, within the bound.
A program may use at most 64 MiB of HBM per device.

```python
import math
import jax
import jax.numpy as jnp
import numpy as np
from jax import lax

HD = 128
KVH = 8
REP = 8
TOK_DEV = 128
REACH = 3
TOKENS = 1024
DOCS = 4


def draw_keys(key, part):
    base = jax.random.truncated_normal(jax.random.fold_in(key, 11), -6.0, 6.0, (TOKENS, KVH, HD), jnp.float32)
    return base.reshape(TOKENS, KVH * HD).astype(jnp.bfloat16)


def draw_queries(key, part):
    base = jax.random.truncated_normal(jax.random.fold_in(key, 21), -6.0, 6.0, (TOKENS, REP, KVH, HD), jnp.float32)
    return base.reshape(TOKENS, REP, KVH * HD).astype(jnp.bfloat16)


def level_of(stream_key, dims, cuts, smallest, top_value):
    level = 1.0
    for dim, shards_of in cuts:
        heights = jax.random.uniform(jax.random.fold_in(jax.random.fold_in(stream_key, 6), dim), (shards_of,), jnp.float32, smallest / len(cuts), top_value / len(cuts))
        level = level * jnp.repeat(jnp.exp(heights), dims[dim] // shards_of).reshape((-1,) + (1,) * (len(dims) - 1 - dim))
    return level


def length_profile(count, total, most, slope):
    weights = [(1 << 20) // math.isqrt(rank ** slope) + 1 for rank in range(2, count + 1)]
    rest, holding = total - most - (count - 1), [1] * (count - 1)
    while rest > 0:
        free = [i for i in range(count - 1) if holding[i] < most]
        pool, remaining = sum([weights[i] for i in free]), rest
        for i in free:
            more = min(most - holding[i], max(1, remaining * weights[i] // pool), rest)
            holding[i] = holding[i] + more
            rest = rest - more
    return np.array([most] + holding)


def ragged_sizes(own_key, number_of, total, most, skew):
    if number_of == 2:
        one = jax.random.randint(own_key, (), max(1, total - most), min(most, total - 1) + 1)
        return jnp.stack([one, total - one])
    sizes = jnp.asarray(length_profile(number_of, total, most, skew), jnp.int32)
    twos = (number_of - 1) // 2
    donor, taker = sizes[1:1 + 2 * twos:2], sizes[2:2 + 2 * twos:2]
    margin = jnp.minimum(donor - 1, most - taker)
    shifted = jax.random.randint(jax.random.fold_in(own_key, 1), (twos,), 0, 1 << 20) % (margin + 1)
    sizes = sizes.at[1:1 + 2 * twos:2].set(donor - shifted).at[2:2 + 2 * twos:2].set(taker + shifted)
    return sizes[jax.random.permutation(jax.random.fold_in(own_key, 2), number_of)]


def scatter_about(rng, extent, scale, reach, split=(), held_as=jnp.bfloat16):
    array = scale * jax.random.normal(rng, extent, jnp.float32)
    if split:
        array = array * level_of(rng, extent, split, -0.22, 0.18)
    return jnp.clip(array, -reach, reach).astype(held_as)


def setup_inputs(seed: int = 0) -> dict:
    key_of = jax.random.split(jax.random.key(seed), 6)
    queries = draw_queries(jax.random.fold_in(key_of[5], 71), 0)
    keys = draw_keys(jax.random.fold_in(key_of[5], 71), 0)
    values = scatter_about(key_of[2], (TOKENS, KVH * HD), 1.0, 6.0, ((0, 8), (1, 4)))
    out_grad = scatter_about(key_of[3], (TOKENS, REP, KVH * HD), 1.0, 6.0, ((0, 8), (1, 4)))
    doc_ids = jnp.searchsorted(jnp.cumsum(ragged_sizes(key_of[4], DOCS, TOKENS, REACH * TOK_DEV, 2)), jnp.arange(TOKENS), side="right").astype(jnp.int32)
    return dict(queries=queries, keys=keys, values=values, out_grad=out_grad, doc_ids=doc_ids)


def window_terms(query_blk, grad_blk, key_win, value_win, seg_rows, seg_keys):
    rows_n = query_blk.shape[0]
    width = key_win.shape[0]
    scale = 1.0 / math.sqrt(HD)
    query_f = query_blk.astype(jnp.float32).reshape(rows_n, REP, KVH, HD)
    grad_f = grad_blk.astype(jnp.float32).reshape(rows_n, REP, KVH, HD)
    key_f = key_win.astype(jnp.float32).reshape(width, KVH, HD)
    value_f = value_win.astype(jnp.float32).reshape(width, KVH, HD)
    row_pos = jnp.arange(rows_n, dtype=jnp.int32)[:, None] + (width - rows_n)
    col_pos = jnp.arange(width, dtype=jnp.int32)[None, :]
    allowed = (seg_rows[:, None] == seg_keys[None, :]) & (col_pos <= row_pos)
    scores = jnp.einsum('trgd,ugd->grtu', query_f, key_f) * scale
    scores = jnp.where(allowed, scores, -1e+30)
    row_max = lax.optimization_barrier(jnp.max(scores, axis=-1, keepdims=True))
    expo = jnp.where(allowed, jnp.exp(scores - row_max), 0.0)
    probs = expo / lax.optimization_barrier(jnp.sum(expo, axis=-1, keepdims=True))
    probs_b = lax.optimization_barrier(probs.astype(jnp.bfloat16)).astype(jnp.float32)
    attended = jnp.einsum('grtu,ugd->trgd', probs_b, value_f).astype(jnp.bfloat16)
    dprob = jnp.einsum('trgd,ugd->grtu', grad_f, value_f)
    delta = lax.optimization_barrier(jnp.sum(probs * dprob, axis=-1, keepdims=True))
    dscore = lax.optimization_barrier((probs * (dprob - delta) * scale).astype(jnp.bfloat16)).astype(jnp.float32)
    query_grad = jnp.einsum('grtu,ugd->trgd', dscore, key_f).astype(jnp.bfloat16)
    key_grad = jnp.einsum('grtu,trgd->ugd', dscore, query_f)
    value_grad = jnp.einsum('grtu,trgd->ugd', probs_b, grad_f)
    return (attended.reshape(rows_n, REP, KVH * HD), query_grad.reshape(rows_n, REP, KVH * HD), key_grad.reshape(width, KVH * HD), value_grad.reshape(width, KVH * HD))

def reference(queries, keys, values, out_grad, doc_ids):
    rows_n = TOK_DEV
    blocks = TOKENS // rows_n
    width = (REACH + 1) * rows_n
    key_pad = jnp.concatenate([jnp.zeros((REACH * rows_n, KVH * HD), jnp.bfloat16), keys], axis=0)
    value_pad = jnp.concatenate([jnp.zeros((REACH * rows_n, KVH * HD), jnp.bfloat16), values], axis=0)
    seg_pad = jnp.concatenate([jnp.full((REACH * rows_n,), -1, jnp.int32), doc_ids.astype(jnp.int32)], axis=0)

    def one_block(index):
        start = (index * rows_n).astype(jnp.int32)
        query_blk = lax.dynamic_slice_in_dim(queries, start, rows_n, 0)
        grad_blk = lax.dynamic_slice_in_dim(out_grad, start, rows_n, 0)
        seg_rows = lax.dynamic_slice_in_dim(doc_ids.astype(jnp.int32), start, rows_n, 0)
        key_win = lax.dynamic_slice_in_dim(key_pad, start, width, 0)
        value_win = lax.dynamic_slice_in_dim(value_pad, start, width, 0)
        seg_keys = lax.dynamic_slice_in_dim(seg_pad, start, width, 0)
        return window_terms(query_blk, grad_blk, key_win, value_win, seg_rows, seg_keys)
    attended, query_grad, key_win_grad, value_win_grad = lax.map(one_block, jnp.arange(blocks, dtype=jnp.int32))

    def combine(window_grad):
        total = window_grad[:, REACH * rows_n:]
        for step in range(1, REACH + 1):
            piece = window_grad[step:, (REACH - step) * rows_n:(REACH - step + 1) * rows_n]
            filler = jnp.zeros((step, rows_n, KVH * HD), jnp.float32)
            total = total + jnp.concatenate([piece, filler], axis=0)
        return total.reshape(TOKENS, KVH * HD).astype(jnp.bfloat16)
    return (attended.reshape(TOKENS, REP, KVH * HD), query_grad.reshape(TOKENS, REP, KVH * HD), combine(key_win_grad), combine(value_win_grad))
```

```python
import functools
import math

import jax
import jax.numpy as jnp
from jax import lax
from jax.experimental import pallas as pl
from jax.experimental.pallas import tpu as pltpu
from jax.sharding import PartitionSpec as P

HD = 128
REACH = 3
MESH = pl.DeviceIdType.MESH


def partner(index, bits):
    out = index
    place = 1
    while place <= bits:
        if bits & place:
            out = out + place * (1 - 2 * ((index // place) % 2))
        place *= 2
    return out


def kernel(
    n_seq, n_head, reps,
    q_ref, k_ref, v_ref, g_ref, doc_ref,
    att_ref, qg_ref, kg_ref, vg_ref,
    qbuf, gbuf, kwin, vwin, kt, vt, docwin, bias, attbuf, qgbuf, kacc, vacc,
    kg_out, vg_out, kg_in, vg_in,
    halo_send, halo_recv, in_send, in_recv, ret_send, ret_recv, grad_send, grad_recv, local_sem,
):
    seq, head = lax.axis_index("seq"), lax.axis_index("head")
    tok, cols = k_ref.shape
    rows = q_ref.shape[0]
    groups = cols // HD
    steps = range(1, REACH + 1)
    peers = range(1, n_head)

    def block(b):
        return pl.ds(b * tok, tok)

    def lanes(g):
        return pl.ds(g * HD, HD)

    def columns(owner, g):
        return pl.ds(pl.multiple_of(owner * cols + g * HD, HD), HD)

    halo = {}
    for b in steps:
        for i, (src, dst) in enumerate(
            ((k_ref, kwin.at[block(b)]), (v_ref, vwin.at[block(b)]), (doc_ref, docwin.at[b]))
        ):
            halo[b, i] = pltpu.make_async_remote_copy(
                src_ref=src, dst_ref=dst, send_sem=halo_send.at[b - 1, i],
                recv_sem=halo_recv.at[b - 1, i], device_id=(seq + b, head), device_id_type=MESH)
    inward = {}
    outward = {}
    for d in peers:
        other = partner(head, d)
        for g in range(groups):
            for i, (src, dst) in enumerate(((q_ref, qbuf), (g_ref, gbuf))):
                inward[d, g, i] = pltpu.make_async_remote_copy(
                    src_ref=src.at[:, columns(other, g)], dst_ref=dst.at[d, :, lanes(g)],
                    send_sem=in_send.at[d - 1, g, i], recv_sem=in_recv.at[d - 1, g, i],
                    device_id=(seq, other), device_id_type=MESH)
            for i, (src, dst) in enumerate(((attbuf, att_ref), (qgbuf, qg_ref))):
                outward[d, g, i] = pltpu.make_async_remote_copy(
                    src_ref=src.at[d, :, lanes(g)], dst_ref=dst.at[:, columns(head, g)],
                    send_sem=ret_send.at[d - 1, g, i], recv_sem=ret_recv.at[d - 1, g, i],
                    device_id=(seq, other), device_id_type=MESH)
    back = {}
    for b in steps:
        for g in range(groups):
            for i, (src, dst) in enumerate(((vg_out, vg_in), (kg_out, kg_in))):
                back[b, g, i] = pltpu.make_async_remote_copy(
                    src_ref=src.at[b - 1, :, lanes(g)], dst_ref=dst.at[b - 1, :, lanes(g)],
                    send_sem=grad_send.at[b - 1, g, i], recv_sem=grad_recv.at[b - 1, g, i],
                    device_id=(seq - b, head), device_id_type=MESH)

    barrier = pltpu.get_barrier_semaphore()
    for d in peers:
        pl.semaphore_signal(barrier, 1, device_id=(seq, partner(head, d)), device_id_type=MESH)
    count = n_head - 1
    for b in steps:
        @pl.when(seq + b < n_seq)
        def _():
            pl.semaphore_signal(barrier, 1, device_id=(seq + b, head), device_id_type=MESH)

        @pl.when(seq >= b)
        def _():
            pl.semaphore_signal(barrier, 1, device_id=(seq - b, head), device_id_type=MESH)
        count = count + jnp.where(seq + b < n_seq, 1, 0) + jnp.where(seq >= b, 1, 0)

    own = [
        pltpu.make_async_copy(src, dst, local_sem.at[i])
        for i, (src, dst) in enumerate((
            (k_ref, kwin.at[block(0)]), (v_ref, vwin.at[block(0)]), (doc_ref, docwin.at[0]),
            (q_ref.at[:, pl.ds(pl.multiple_of(head * cols, HD), cols)], qbuf.at[0]),
            (g_ref.at[:, pl.ds(pl.multiple_of(head * cols, HD), cols)], gbuf.at[0])))
    ]
    for copy in own:
        copy.start()
    pl.semaphore_wait(barrier, count)

    for b in steps:
        @pl.when(seq + b < n_seq)
        def _():
            for i in (2, 0, 1):
                halo[b, i].start()
    for d in peers:
        for g in range(groups):
            for i in range(2):
                inward[d, g, i].start()

    for b in steps:
        @pl.when(seq < b)
        def _():
            kwin[block(b), :] = jnp.zeros((tok, cols), kwin.dtype)
            vwin[block(b), :] = jnp.zeros((tok, cols), vwin.dtype)
            docwin[b] = jnp.full((1, tok), -1, jnp.int32)

    key_of = lax.broadcasted_iota(jnp.int32, (tok, rows), 0)
    token_of = lax.broadcasted_iota(jnp.int32, (tok, rows), 1) // reps
    near = key_of <= token_of
    for copy in own:
        copy.wait()
    for b in steps:
        @pl.when(seq >= b)
        def _():
            for i in range(3):
                halo[b, i].wait_recv()

    doc_own = docwin[0].astype(jnp.float32)
    if reps == 1:
        doc_q = doc_own
    else:
        spread = (key_of == token_of).astype(jnp.bfloat16)
        doc_q = jnp.dot(jnp.broadcast_to(doc_own, (16, tok)).astype(jnp.bfloat16), spread,
                        preferred_element_type=jnp.float32)[0:1]

    def same(b):
        doc = jnp.transpose(jnp.broadcast_to(docwin[b].astype(jnp.float32), (tok, tok)))
        return jnp.where(doc[:, 0:1] == doc_q, 0.0, -1e30)

    bias[block(0), :] = jnp.where(near, same(0), same(REACH))
    for b in range(1, REACH):
        bias[block(b), :] = same(b)
    for g in range(groups):
        kt[g] = jnp.transpose(kwin[:, lanes(g)])
        vt[g] = jnp.transpose(vwin[:, lanes(g)])

    scale = 1.0 / math.sqrt(HD)
    last = REACH * tok

    def folded(x):
        return jnp.concatenate([jnp.where(near, x[:tok], x[last:]), x[tok:last]], axis=0)

    def unfolded(x):
        zero = jnp.zeros((tok, rows), x.dtype)
        return jnp.concatenate(
            [jnp.where(near, x[:tok], zero), x[tok:], jnp.where(near, zero, x[:tok])], axis=0)

    def tile(d, g):
        q = qbuf[d, :, lanes(g)]
        grad = gbuf[d, :, lanes(g)]
        by_last = (((1,), (1,)), ((), ()))
        s = folded(lax.dot_general(kwin[:, lanes(g)], q, by_last, preferred_element_type=jnp.float32))
        s = s + bias[...]
        top = jnp.max(s, axis=0, keepdims=True)
        e = jnp.exp2((s - top) * (scale * math.log2(math.e)))
        p = e * (1.0 / jnp.sum(e, axis=0, keepdims=True))
        dp = folded(lax.dot_general(vwin[:, lanes(g)], grad, by_last, preferred_element_type=jnp.float32))
        delta = jnp.sum(p * dp, axis=0, keepdims=True)
        ds = unfolded(p * (dp - delta) * scale).astype(jnp.bfloat16)
        pb = unfolded(p).astype(jnp.bfloat16)
        att = jnp.dot(vt[g], pb, preferred_element_type=jnp.float32)
        attbuf[d, :, lanes(g)] = jnp.transpose(att).astype(jnp.bfloat16)
        qg = jnp.dot(kt[g], ds, preferred_element_type=jnp.float32)
        qgbuf[d, :, lanes(g)] = jnp.transpose(qg).astype(jnp.bfloat16)
        dv = jnp.dot(pb, grad, preferred_element_type=jnp.float32)
        dk = jnp.dot(ds, q, preferred_element_type=jnp.float32)
        if d == 0:
            vacc[:, lanes(g)] = dv
            kacc[:, lanes(g)] = dk
        else:
            vacc[:, lanes(g)] += dv
            kacc[:, lanes(g)] += dk

    for d in range(n_head):
        for g in range(groups):
            if d:
                inward[d, g, 0].wait_recv()
                inward[d, g, 1].wait_recv()
            tile(d, g)
            if d:
                outward[d, g, 0].start()
                outward[d, g, 1].start()
            if d == n_head - 1:
                for b in steps:
                    vg_out[b - 1, :, lanes(g)] = vacc[block(b), lanes(g)].astype(jnp.bfloat16)
                    kg_out[b - 1, :, lanes(g)] = kacc[block(b), lanes(g)].astype(jnp.bfloat16)

                    @pl.when(seq >= b)
                    def _():
                        back[b, g, 0].start()
                        back[b, g, 1].start()
        if d == 0:
            mine = pl.ds(pl.multiple_of(head * cols, HD), cols)
            done = [pltpu.make_async_copy(attbuf.at[0], att_ref.at[:, mine], local_sem.at[0]),
                    pltpu.make_async_copy(qgbuf.at[0], qg_ref.at[:, mine], local_sem.at[1])]
            for copy in done:
                copy.start()

    for b in steps:
        @pl.when(seq + b < n_seq)
        def _():
            for g in range(groups):
                for i in range(2):
                    back[b, g, i].wait_recv()
            vacc[block(0), :] += vg_in[b - 1].astype(jnp.float32)
            kacc[block(0), :] += kg_in[b - 1].astype(jnp.float32)
    vg_ref[...] = vacc[block(0), :].astype(vg_ref.dtype)
    kg_ref[...] = kacc[block(0), :].astype(kg_ref.dtype)

    for copy in done:
        copy.wait()
    for b in steps:
        @pl.when(seq + b < n_seq)
        def _():
            for i in range(3):
                halo[b, i].wait_send()

        @pl.when(seq >= b)
        def _():
            for g in range(groups):
                for i in range(2):
                    back[b, g, i].wait_send()
    for d in peers:
        for g in range(groups):
            for i in range(2):
                inward[d, g, i].wait_send()
                outward[d, g, i].wait_send()
                outward[d, g, i].wait_recv()


def on_device(n_seq, n_head, queries, keys, values, out_grad, doc_ids):
    tok, reps, width = queries.shape
    cols = keys.shape[1]
    groups = cols // HD
    rows = tok * reps
    span = (REACH + 1) * tok
    bf16, f32 = jnp.bfloat16, jnp.float32
    dma = pltpu.SemaphoreType.DMA
    anywhere = pl.BlockSpec(memory_space=pl.ANY)
    vmem = pl.BlockSpec(memory_space=pltpu.VMEM)
    flat = jax.ShapeDtypeStruct((rows, width), bf16)
    narrow = jax.ShapeDtypeStruct((tok, cols), bf16)
    att, qg, kg, vg = pl.pallas_call(
        functools.partial(kernel, n_seq, n_head, reps),
        out_shape=(flat, flat, narrow, narrow),
        in_specs=[anywhere] * 5,
        out_specs=(anywhere, anywhere, vmem, vmem),
        scratch_shapes=[
            pltpu.VMEM((n_head, rows, cols), bf16),
            pltpu.VMEM((n_head, rows, cols), bf16),
            pltpu.VMEM((span, cols), bf16),
            pltpu.VMEM((span, cols), bf16),
            pltpu.VMEM((groups, HD, span), bf16),
            pltpu.VMEM((groups, HD, span), bf16),
            pltpu.VMEM((REACH + 1, 1, tok), jnp.int32),
            pltpu.VMEM((REACH * tok, rows), f32),
            pltpu.VMEM((n_head, rows, cols), bf16),
            pltpu.VMEM((n_head, rows, cols), bf16),
            pltpu.VMEM((span, cols), f32),
            pltpu.VMEM((span, cols), f32),
            pltpu.VMEM((REACH, tok, cols), bf16),
            pltpu.VMEM((REACH, tok, cols), bf16),
            pltpu.VMEM((REACH, tok, cols), bf16),
            pltpu.VMEM((REACH, tok, cols), bf16),
            dma((REACH, 3)), dma((REACH, 3)),
            dma((n_head - 1, groups, 2)), dma((n_head - 1, groups, 2)),
            dma((n_head - 1, groups, 2)), dma((n_head - 1, groups, 2)),
            dma((REACH, groups, 2)), dma((REACH, groups, 2)),
            dma((5,)),
        ],
        compiler_params=pltpu.CompilerParams(
            collective_id=0, has_side_effects=True, vmem_limit_bytes=32 * 2**20),
        cost_estimate=pl.CostEstimate(
            flops=12 * n_head * groups * rows * span * HD,
            bytes_accessed=8 * rows * width + 8 * tok * cols,
            transcendentals=n_head * groups * rows * REACH * tok),
        name="attention_layer",
    )(queries.reshape(rows, width), keys, values, out_grad.reshape(rows, width), doc_ids.reshape(1, tok))
    return (att.reshape(tok, reps, width), qg.reshape(tok, reps, width), kg, vg)


def solution(mesh):
    wide, thin = P("seq", "head", None), P("seq", "head")
    return jax.shard_map(
        functools.partial(on_device, mesh.shape["seq"], mesh.shape["head"]),
        mesh=mesh, in_specs=(wide, thin, thin, wide, P("seq")),
        out_specs=(wide, wide, thin, thin), check_vma=False)
```

```python
import functools
import math

import jax
import jax.numpy as jnp
from jax import lax
from jax.experimental import pallas as pl
from jax.experimental.pallas import tpu as pltpu
from jax.sharding import PartitionSpec as P

HD = 128
REACH = 3
MESH = pl.DeviceIdType.MESH


def partner(index, bits):
    out = index
    place = 1
    while place <= bits:
        if bits & place:
            out = out + place * (1 - 2 * ((index // place) % 2))
        place *= 2
    return out


def kernel(
    n_seq, n_head, reps,
    q_ref, k_ref, v_ref, g_ref, doc_ref,
    att_ref, qg_ref, kg_ref, vg_ref,
    qbuf, gbuf, kwin, vwin, kt, vt, docwin, bias, attbuf, qgbuf, kacc, vacc,
    kg_out, vg_out, kg_in, vg_in,
    halo_send, halo_recv, in_send, in_recv, ret_send, ret_recv, grad_send, grad_recv, local_sem,
):
    seq, head = lax.axis_index("seq"), lax.axis_index("head")
    tok, cols = k_ref.shape
    rows = q_ref.shape[0]
    groups = cols // HD
    steps = range(1, REACH + 1)
    peers = range(1, n_head)

    def block(b):
        return pl.ds(b * tok, tok)

    def lanes(g):
        return pl.ds(g * HD, HD)

    def columns(owner, g):
        return pl.ds(pl.multiple_of(owner * cols + g * HD, HD), HD)

    halo = {}
    for b in steps:
        pairs = [(doc_ref, docwin.at[b])]
        for g in range(groups):
            pairs.append((k_ref.at[:, lanes(g)], kwin.at[block(b), lanes(g)]))
            pairs.append((v_ref.at[:, lanes(g)], vwin.at[block(b), lanes(g)]))
        for i, (src, dst) in enumerate(pairs):
            halo[b, i] = pltpu.make_async_remote_copy(
                src_ref=src, dst_ref=dst, send_sem=halo_send.at[b - 1, i],
                recv_sem=halo_recv.at[b - 1, i], device_id=(seq + b, head), device_id_type=MESH)
    halos = 1 + 2 * groups
    inward = {}
    outward = {}
    for d in peers:
        other = partner(head, d)
        for g in range(groups):
            for i, (src, dst) in enumerate(((q_ref, qbuf), (g_ref, gbuf))):
                inward[d, g, i] = pltpu.make_async_remote_copy(
                    src_ref=src.at[:, columns(other, g)], dst_ref=dst.at[d, :, lanes(g)],
                    send_sem=in_send.at[d - 1, g, i], recv_sem=in_recv.at[d - 1, g, i],
                    device_id=(seq, other), device_id_type=MESH)
            for i, (src, dst) in enumerate(((attbuf, att_ref), (qgbuf, qg_ref))):
                outward[d, g, i] = pltpu.make_async_remote_copy(
                    src_ref=src.at[d, :, lanes(g)], dst_ref=dst.at[:, columns(head, g)],
                    send_sem=ret_send.at[d - 1, g, i], recv_sem=ret_recv.at[d - 1, g, i],
                    device_id=(seq, other), device_id_type=MESH)
    back = {}
    for b in steps:
        for g in range(groups):
            for i, (src, dst) in enumerate(((vg_out, vg_in), (kg_out, kg_in))):
                back[b, g, i] = pltpu.make_async_remote_copy(
                    src_ref=src.at[b - 1, :, lanes(g)], dst_ref=dst.at[b - 1, :, lanes(g)],
                    send_sem=grad_send.at[b - 1, g, i], recv_sem=grad_recv.at[b - 1, g, i],
                    device_id=(seq - b, head), device_id_type=MESH)

    barrier = pltpu.get_barrier_semaphore()
    for d in peers:
        pl.semaphore_signal(barrier, 1, device_id=(seq, partner(head, d)), device_id_type=MESH)
    count = n_head - 1
    for b in steps:
        @pl.when(seq + b < n_seq)
        def _():
            pl.semaphore_signal(barrier, 1, device_id=(seq + b, head), device_id_type=MESH)

        @pl.when(seq >= b)
        def _():
            pl.semaphore_signal(barrier, 1, device_id=(seq - b, head), device_id_type=MESH)
        count = count + jnp.where(seq + b < n_seq, 1, 0) + jnp.where(seq >= b, 1, 0)

    own = [
        pltpu.make_async_copy(src, dst, local_sem.at[i])
        for i, (src, dst) in enumerate((
            (k_ref, kwin.at[block(0)]), (v_ref, vwin.at[block(0)]), (doc_ref, docwin.at[0]),
            (q_ref.at[:, pl.ds(pl.multiple_of(head * cols, HD), cols)], qbuf.at[0]),
            (g_ref.at[:, pl.ds(pl.multiple_of(head * cols, HD), cols)], gbuf.at[0])))
    ]
    for copy in own:
        copy.start()
    pl.semaphore_wait(barrier, count)

    for g in range(groups):
        for b in reversed(steps):
            @pl.when(seq + b < n_seq)
            def _():
                for i in ((0, 1, 2) if g == 0 else (1 + 2 * g, 2 + 2 * g)):
                    halo[b, i].start()
        for d in reversed(peers):
            for i in range(2):
                inward[d, g, i].start()

    for b in steps:
        @pl.when(seq < b)
        def _():
            kwin[block(b), :] = jnp.zeros((tok, cols), kwin.dtype)
            vwin[block(b), :] = jnp.zeros((tok, cols), vwin.dtype)
            docwin[b] = jnp.full((1, tok), -1, jnp.int32)

    key_of = lax.broadcasted_iota(jnp.int32, (tok, rows), 0)
    token_of = lax.broadcasted_iota(jnp.int32, (tok, rows), 1) // reps
    near = key_of <= token_of
    for copy in own:
        copy.wait()
    for b in steps:
        @pl.when(seq >= b)
        def _():
            halo[b, 0].wait_recv()

    doc_own = docwin[0].astype(jnp.float32)
    if reps == 1:
        doc_q = doc_own
    else:
        spread = (key_of == token_of).astype(jnp.bfloat16)
        doc_q = jnp.dot(jnp.broadcast_to(doc_own, (16, tok)).astype(jnp.bfloat16), spread,
                        preferred_element_type=jnp.float32)[0:1]

    def same(b):
        doc = jnp.transpose(jnp.broadcast_to(docwin[b].astype(jnp.float32), (tok, tok)))
        return jnp.where(doc[:, 0:1] == doc_q, 0.0, -1e30)

    bias[block(0), :] = jnp.where(near, same(0), same(REACH))
    for b in range(1, REACH):
        bias[block(b), :] = same(b)

    scale = 1.0 / math.sqrt(HD)
    last = REACH * tok

    def folded(x):
        return jnp.concatenate([jnp.where(near, x[:tok], x[last:]), x[tok:last]], axis=0)

    def unfolded(x):
        zero = jnp.zeros((tok, rows), x.dtype)
        return jnp.concatenate(
            [jnp.where(near, x[:tok], zero), x[tok:], jnp.where(near, zero, x[:tok])], axis=0)

    def tile(d, g):
        q = qbuf[d, :, lanes(g)]
        grad = gbuf[d, :, lanes(g)]
        by_last = (((1,), (1,)), ((), ()))
        s = folded(lax.dot_general(kwin[:, lanes(g)], q, by_last, preferred_element_type=jnp.float32))
        s = s + bias[...]
        top = jnp.max(s, axis=0, keepdims=True)
        e = jnp.exp2((s - top) * (scale * math.log2(math.e)))
        p = e * (1.0 / jnp.sum(e, axis=0, keepdims=True))
        dp = folded(lax.dot_general(vwin[:, lanes(g)], grad, by_last, preferred_element_type=jnp.float32))
        delta = jnp.sum(p * dp, axis=0, keepdims=True)
        ds = unfolded(p * (dp - delta) * scale).astype(jnp.bfloat16)
        pb = unfolded(p).astype(jnp.bfloat16)
        att = jnp.dot(vt[g], pb, preferred_element_type=jnp.float32)
        attbuf[d, :, lanes(g)] = jnp.transpose(att).astype(jnp.bfloat16)
        qg = jnp.dot(kt[g], ds, preferred_element_type=jnp.float32)
        qgbuf[d, :, lanes(g)] = jnp.transpose(qg).astype(jnp.bfloat16)
        dv = jnp.dot(pb, grad, preferred_element_type=jnp.float32)
        dk = jnp.dot(ds, q, preferred_element_type=jnp.float32)
        if d == 0:
            vacc[:, lanes(g)] = dv
            kacc[:, lanes(g)] = dk
        else:
            vacc[:, lanes(g)] += dv
            kacc[:, lanes(g)] += dk

    mine = pl.ds(pl.multiple_of(head * cols, HD), cols)
    done = [pltpu.make_async_copy(attbuf.at[0], att_ref.at[:, mine], local_sem.at[0]),
            pltpu.make_async_copy(qgbuf.at[0], qg_ref.at[:, mine], local_sem.at[1])]
    for g in range(groups):
        for b in steps:
            @pl.when(seq >= b)
            def _():
                halo[b, 1 + 2 * g].wait_recv()
                halo[b, 2 + 2 * g].wait_recv()
        kt[g] = jnp.transpose(kwin[:, lanes(g)])
        vt[g] = jnp.transpose(vwin[:, lanes(g)])
        for d in range(n_head):
            if d:
                inward[d, g, 0].wait_recv()
                inward[d, g, 1].wait_recv()
            tile(d, g)
            if d:
                outward[d, g, 0].start()
                outward[d, g, 1].start()
            elif g == groups - 1:
                for copy in done:
                    copy.start()
        for b in reversed(steps):
            vg_out[b - 1, :, lanes(g)] = vacc[block(b), lanes(g)].astype(jnp.bfloat16)
            kg_out[b - 1, :, lanes(g)] = kacc[block(b), lanes(g)].astype(jnp.bfloat16)

            @pl.when(seq >= b)
            def _():
                back[b, g, 0].start()
                back[b, g, 1].start()

    for b in steps:
        @pl.when(seq + b < n_seq)
        def _():
            for g in range(groups):
                for i in range(2):
                    back[b, g, i].wait_recv()
            vacc[block(0), :] += vg_in[b - 1].astype(jnp.float32)
            kacc[block(0), :] += kg_in[b - 1].astype(jnp.float32)
    vg_ref[...] = vacc[block(0), :].astype(vg_ref.dtype)
    kg_ref[...] = kacc[block(0), :].astype(kg_ref.dtype)

    for copy in done:
        copy.wait()
    for b in steps:
        @pl.when(seq + b < n_seq)
        def _():
            for i in range(halos):
                halo[b, i].wait_send()

        @pl.when(seq >= b)
        def _():
            for g in range(groups):
                for i in range(2):
                    back[b, g, i].wait_send()
    for d in peers:
        for g in range(groups):
            for i in range(2):
                inward[d, g, i].wait_send()
                outward[d, g, i].wait_send()
                outward[d, g, i].wait_recv()


def on_device(n_seq, n_head, queries, keys, values, out_grad, doc_ids):
    tok, reps, width = queries.shape
    cols = keys.shape[1]
    groups = cols // HD
    rows = tok * reps
    span = (REACH + 1) * tok
    bf16, f32 = jnp.bfloat16, jnp.float32
    dma = pltpu.SemaphoreType.DMA
    anywhere = pl.BlockSpec(memory_space=pl.ANY)
    vmem = pl.BlockSpec(memory_space=pltpu.VMEM)
    flat = jax.ShapeDtypeStruct((rows, width), bf16)
    narrow = jax.ShapeDtypeStruct((tok, cols), bf16)
    att, qg, kg, vg = pl.pallas_call(
        functools.partial(kernel, n_seq, n_head, reps),
        out_shape=(flat, flat, narrow, narrow),
        in_specs=[anywhere] * 5,
        out_specs=(anywhere, anywhere, vmem, vmem),
        scratch_shapes=[
            pltpu.VMEM((n_head, rows, cols), bf16),
            pltpu.VMEM((n_head, rows, cols), bf16),
            pltpu.VMEM((span, cols), bf16),
            pltpu.VMEM((span, cols), bf16),
            pltpu.VMEM((groups, HD, span), bf16),
            pltpu.VMEM((groups, HD, span), bf16),
            pltpu.VMEM((REACH + 1, 1, tok), jnp.int32),
            pltpu.VMEM((REACH * tok, rows), f32),
            pltpu.VMEM((n_head, rows, cols), bf16),
            pltpu.VMEM((n_head, rows, cols), bf16),
            pltpu.VMEM((span, cols), f32),
            pltpu.VMEM((span, cols), f32),
            pltpu.VMEM((REACH, tok, cols), bf16),
            pltpu.VMEM((REACH, tok, cols), bf16),
            pltpu.VMEM((REACH, tok, cols), bf16),
            pltpu.VMEM((REACH, tok, cols), bf16),
            dma((REACH, 1 + 2 * groups)), dma((REACH, 1 + 2 * groups)),
            dma((n_head - 1, groups, 2)), dma((n_head - 1, groups, 2)),
            dma((n_head - 1, groups, 2)), dma((n_head - 1, groups, 2)),
            dma((REACH, groups, 2)), dma((REACH, groups, 2)),
            dma((5,)),
        ],
        compiler_params=pltpu.CompilerParams(
            collective_id=0, has_side_effects=True, vmem_limit_bytes=32 * 2**20),
        cost_estimate=pl.CostEstimate(
            flops=12 * n_head * groups * rows * span * HD,
            bytes_accessed=8 * rows * width + 8 * tok * cols,
            transcendentals=n_head * groups * rows * REACH * tok),
        name="attention_layer",
    )(queries.reshape(rows, width), keys, values, out_grad.reshape(rows, width), doc_ids.reshape(1, tok))
    return (att.reshape(tok, reps, width), qg.reshape(tok, reps, width), kg, vg)


def solution(mesh):
    wide, thin = P("seq", "head", None), P("seq", "head")
    return jax.shard_map(
        functools.partial(on_device, mesh.shape["seq"], mesh.shape["head"]),
        mesh=mesh, in_specs=(wide, thin, thin, wide, P("seq")),
        out_specs=(wide, wide, thin, thin), check_vma=False)
```

```python
import functools
import math

import jax
import jax.numpy as jnp
from jax import lax
from jax.experimental import pallas as pl
from jax.experimental.pallas import tpu as pltpu
from jax.sharding import PartitionSpec as P

HD = 128
REACH = 3
LIMIT = 60 * 2**20
MESH = pl.DeviceIdType.MESH


def partner(index, bits):
    out = index
    place = 1
    while place <= bits:
        if bits & place:
            out = out + place * (1 - 2 * ((index // place) % 2))
        place *= 2
    return out


def kernel(
    n_seq, n_head, reps,
    q_ref, k_ref, v_ref, g_ref, doc_ref,
    att_ref, qg_ref, kg_ref, vg_ref,
    qbuf, gbuf, kwin, vwin, kt, vt, docwin, bias, attbuf, qgbuf, kacc, vacc,
    kg_out, vg_out, kg_in, vg_in,
    halo_send, halo_recv, in_send, in_recv, ret_send, ret_recv, grad_send, grad_recv, local_sem,
):
    seq, head = lax.axis_index("seq"), lax.axis_index("head")
    tok, cols = k_ref.shape
    rows = tok * reps
    groups = cols // HD
    steps = range(1, REACH + 1)
    peers = range(1, n_head)

    def block(b):
        return pl.ds(b * tok, tok)

    def lanes(g):
        return pl.ds(g * HD, HD)

    def columns(ref, owner, g):
        at = pl.ds(pl.multiple_of(owner * cols + g * HD, HD), HD)
        return ref.at[:, at] if len(ref.shape) == 2 else ref.at[:, :, at]

    def matrix(ref, d, g):
        view = ref.at[d, g]
        return view if len(view.shape) == 2 else view.reshape(rows, HD)

    halo = {}
    for b in steps:
        pairs = [(doc_ref, docwin.at[b])]
        for g in range(groups):
            pairs.append((k_ref.at[:, lanes(g)], kwin.at[block(b), lanes(g)]))
            pairs.append((v_ref.at[:, lanes(g)], vwin.at[block(b), lanes(g)]))
        for i, (src, dst) in enumerate(pairs):
            halo[b, i] = pltpu.make_async_remote_copy(
                src_ref=src, dst_ref=dst, send_sem=halo_send.at[b - 1, i],
                recv_sem=halo_recv.at[b - 1, i], device_id=(seq + b, head), device_id_type=MESH)
    halos = 1 + 2 * groups
    inward = {}
    outward = {}
    for d in peers:
        other = partner(head, d)
        for g in range(groups):
            for i, (src, dst) in enumerate(((q_ref, qbuf), (g_ref, gbuf))):
                inward[d, g, i] = pltpu.make_async_remote_copy(
                    src_ref=columns(src, other, g), dst_ref=dst.at[d, g],
                    send_sem=in_send.at[d - 1, g, i], recv_sem=in_recv.at[d - 1, g, i],
                    device_id=(seq, other), device_id_type=MESH)
            for i, (src, dst) in enumerate(((attbuf, att_ref), (qgbuf, qg_ref))):
                outward[d, g, i] = pltpu.make_async_remote_copy(
                    src_ref=src.at[d, g], dst_ref=columns(dst, head, g),
                    send_sem=ret_send.at[d - 1, g, i], recv_sem=ret_recv.at[d - 1, g, i],
                    device_id=(seq, other), device_id_type=MESH)
    back = {}
    for b in steps:
        for g in range(groups):
            for i, (src, dst) in enumerate(((vg_out, vg_in), (kg_out, kg_in))):
                back[b, g, i] = pltpu.make_async_remote_copy(
                    src_ref=src.at[b - 1, :, lanes(g)], dst_ref=dst.at[b - 1, :, lanes(g)],
                    send_sem=grad_send.at[b - 1, g, i], recv_sem=grad_recv.at[b - 1, g, i],
                    device_id=(seq - b, head), device_id_type=MESH)

    barrier = pltpu.get_barrier_semaphore()
    for d in peers:
        pl.semaphore_signal(barrier, 1, device_id=(seq, partner(head, d)), device_id_type=MESH)
    count = n_head - 1
    for b in steps:
        @pl.when(seq + b < n_seq)
        def _():
            pl.semaphore_signal(barrier, 1, device_id=(seq + b, head), device_id_type=MESH)

        @pl.when(seq >= b)
        def _():
            pl.semaphore_signal(barrier, 1, device_id=(seq - b, head), device_id_type=MESH)
        count = count + jnp.where(seq + b < n_seq, 1, 0) + jnp.where(seq >= b, 1, 0)

    own = [
        pltpu.make_async_copy(src, dst, local_sem.at[i])
        for i, (src, dst) in enumerate(
            [(k_ref, kwin.at[block(0)]), (v_ref, vwin.at[block(0)]), (doc_ref, docwin.at[0])]
            + [(columns(q_ref, head, g), qbuf.at[0, g]) for g in range(groups)]
            + [(columns(g_ref, head, g), gbuf.at[0, g]) for g in range(groups)])
    ]
    for copy in own:
        copy.start()
    pl.semaphore_wait(barrier, count)

    for g in range(groups):
        for b in reversed(steps):
            @pl.when(seq + b < n_seq)
            def _():
                for i in ((0, 1, 2) if g == 0 else (1 + 2 * g, 2 + 2 * g)):
                    halo[b, i].start()
        for d in reversed(peers):
            for i in range(2):
                inward[d, g, i].start()

    for b in steps:
        @pl.when(seq < b)
        def _():
            kwin[block(b), :] = jnp.zeros((tok, cols), kwin.dtype)
            vwin[block(b), :] = jnp.zeros((tok, cols), vwin.dtype)
            docwin[b] = jnp.full((1, tok), -1, jnp.int32)

    key_of = lax.broadcasted_iota(jnp.int32, (tok, rows), 0)
    token_of = lax.broadcasted_iota(jnp.int32, (tok, rows), 1) // reps
    near = key_of <= token_of
    for copy in own:
        copy.wait()
    for b in steps:
        @pl.when(seq >= b)
        def _():
            halo[b, 0].wait_recv()

    doc_own = docwin[0].astype(jnp.float32)
    if reps == 1:
        doc_q = doc_own
    else:
        spread = (key_of == token_of).astype(jnp.bfloat16)
        doc_q = jnp.dot(jnp.broadcast_to(doc_own, (16, tok)).astype(jnp.bfloat16), spread,
                        preferred_element_type=jnp.float32)[0:1]

    def same(b):
        doc = jnp.transpose(jnp.broadcast_to(docwin[b].astype(jnp.float32), (tok, tok)))
        return jnp.where(doc[:, 0:1] == doc_q, 0.0, -1e30)

    bias[block(0), :] = jnp.where(near, same(0), same(REACH))
    for b in range(1, REACH):
        bias[block(b), :] = same(b)

    scale = 1.0 / math.sqrt(HD)
    last = REACH * tok

    def folded(x):
        return jnp.concatenate([jnp.where(near, x[:tok], x[last:]), x[tok:last]], axis=0)

    def unfolded(x):
        zero = jnp.zeros((tok, rows), x.dtype)
        return jnp.concatenate(
            [jnp.where(near, x[:tok], zero), x[tok:], jnp.where(near, zero, x[:tok])], axis=0)

    def tile(d, g):
        q = matrix(qbuf, d, g)[...]
        grad = matrix(gbuf, d, g)[...]
        by_last = (((1,), (1,)), ((), ()))
        s = folded(lax.dot_general(kwin[:, lanes(g)], q, by_last, preferred_element_type=jnp.float32))
        s = s + bias[...]
        top = jnp.max(s, axis=0, keepdims=True)
        e = jnp.exp2((s - top) * (scale * math.log2(math.e)))
        p = e * (1.0 / jnp.sum(e, axis=0, keepdims=True))
        dp = folded(lax.dot_general(vwin[:, lanes(g)], grad, by_last, preferred_element_type=jnp.float32))
        delta = jnp.sum(p * dp, axis=0, keepdims=True)
        ds = unfolded(p * (dp - delta) * scale).astype(jnp.bfloat16)
        pb = unfolded(p).astype(jnp.bfloat16)
        att = jnp.dot(vt[g], pb, preferred_element_type=jnp.float32)
        matrix(attbuf, d, g)[...] = jnp.transpose(att).astype(jnp.bfloat16)
        qg = jnp.dot(kt[g], ds, preferred_element_type=jnp.float32)
        matrix(qgbuf, d, g)[...] = jnp.transpose(qg).astype(jnp.bfloat16)
        dv = jnp.dot(pb, grad, preferred_element_type=jnp.float32)
        dk = jnp.dot(ds, q, preferred_element_type=jnp.float32)
        if d == 0:
            vacc[:, lanes(g)] = dv
            kacc[:, lanes(g)] = dk
        else:
            vacc[:, lanes(g)] += dv
            kacc[:, lanes(g)] += dk

    done = [pltpu.make_async_copy(src.at[0, g], columns(dst, head, g), local_sem.at[2 * g + i])
            for g in range(groups) for i, (src, dst) in enumerate(((attbuf, att_ref), (qgbuf, qg_ref)))]
    for g in range(groups):
        for b in steps:
            @pl.when(seq >= b)
            def _():
                halo[b, 1 + 2 * g].wait_recv()
                halo[b, 2 + 2 * g].wait_recv()
        kt[g] = jnp.transpose(kwin[:, lanes(g)])
        vt[g] = jnp.transpose(vwin[:, lanes(g)])
        for d in range(n_head):
            if d:
                inward[d, g, 0].wait_recv()
                inward[d, g, 1].wait_recv()
            tile(d, g)
            if d:
                outward[d, g, 0].start()
                outward[d, g, 1].start()
            else:
                done[2 * g].start()
                done[2 * g + 1].start()
        for b in reversed(steps):
            vg_out[b - 1, :, lanes(g)] = vacc[block(b), lanes(g)].astype(jnp.bfloat16)
            kg_out[b - 1, :, lanes(g)] = kacc[block(b), lanes(g)].astype(jnp.bfloat16)

            @pl.when(seq >= b)
            def _():
                back[b, g, 0].start()
                back[b, g, 1].start()

    for b in steps:
        @pl.when(seq + b < n_seq)
        def _():
            for g in range(groups):
                for i in range(2):
                    back[b, g, i].wait_recv()
            vacc[block(0), :] += vg_in[b - 1].astype(jnp.float32)
            kacc[block(0), :] += kg_in[b - 1].astype(jnp.float32)
    vg_ref[...] = vacc[block(0), :].astype(vg_ref.dtype)
    kg_ref[...] = kacc[block(0), :].astype(kg_ref.dtype)

    for copy in done:
        copy.wait()
    for b in steps:
        @pl.when(seq + b < n_seq)
        def _():
            for i in range(halos):
                halo[b, i].wait_send()

        @pl.when(seq >= b)
        def _():
            for g in range(groups):
                for i in range(2):
                    back[b, g, i].wait_send()
    for d in peers:
        for g in range(groups):
            for i in range(2):
                inward[d, g, i].wait_send()
                outward[d, g, i].wait_send()
                outward[d, g, i].wait_recv()


def settle(*refs):
    sources, places, sem = refs[:4], refs[4:8], refs[8]
    copies = []
    for src, dst in zip(sources, places):
        parts = 4 if len(copies) < 8 else 1
        size = src.shape[0] // parts
        for part in range(parts):
            at = pl.ds(part * size, size)
            copies.append(pltpu.make_async_copy(src.at[at], dst.at[at], sem.at[len(copies)]))
    for copy in copies:
        copy.start()
    for copy in copies:
        copy.wait()


def on_device(n_seq, n_head, queries, keys, values, out_grad, doc_ids):
    tok, reps, width = queries.shape
    cols = keys.shape[1]
    groups = cols // HD
    rows = tok * reps
    span = (REACH + 1) * tok
    whole = (tok, reps, width) if reps > 1 else (tok, width)
    piece = whole[:-1] + (HD,)
    bf16, f32 = jnp.bfloat16, jnp.float32
    dma = pltpu.SemaphoreType.DMA
    anywhere = pl.BlockSpec(memory_space=pl.ANY)
    vmem = pl.BlockSpec(memory_space=pltpu.VMEM)
    flat = jax.ShapeDtypeStruct(whole, bf16)
    narrow = jax.ShapeDtypeStruct((tok, cols), bf16)
    results = pl.pallas_call(
        functools.partial(kernel, n_seq, n_head, reps),
        out_shape=(flat, flat, narrow, narrow),
        in_specs=[anywhere] * 5,
        out_specs=(anywhere, anywhere, vmem, vmem),
        scratch_shapes=[
            pltpu.VMEM((n_head, groups) + piece, bf16),
            pltpu.VMEM((n_head, groups) + piece, bf16),
            pltpu.VMEM((span, cols), bf16),
            pltpu.VMEM((span, cols), bf16),
            pltpu.VMEM((groups, HD, span), bf16),
            pltpu.VMEM((groups, HD, span), bf16),
            pltpu.VMEM((REACH + 1, 1, tok), jnp.int32),
            pltpu.VMEM((REACH * tok, rows), f32),
            pltpu.VMEM((n_head, groups) + piece, bf16),
            pltpu.VMEM((n_head, groups) + piece, bf16),
            pltpu.VMEM((span, cols), f32),
            pltpu.VMEM((span, cols), f32),
            pltpu.VMEM((REACH, tok, cols), bf16),
            pltpu.VMEM((REACH, tok, cols), bf16),
            pltpu.VMEM((REACH, tok, cols), bf16),
            pltpu.VMEM((REACH, tok, cols), bf16),
            dma((REACH, 1 + 2 * groups)), dma((REACH, 1 + 2 * groups)),
            dma((n_head - 1, groups, 2)), dma((n_head - 1, groups, 2)),
            dma((n_head - 1, groups, 2)), dma((n_head - 1, groups, 2)),
            dma((REACH, groups, 2)), dma((REACH, groups, 2)),
            dma((3 + 2 * groups,)),
        ],
        compiler_params=pltpu.CompilerParams(
            collective_id=0, has_side_effects=True, vmem_limit_bytes=LIMIT),
        cost_estimate=pl.CostEstimate(
            flops=12 * n_head * groups * rows * span * HD,
            bytes_accessed=8 * rows * width + 8 * tok * cols,
            transcendentals=n_head * groups * rows * REACH * tok),
        name="attention_layer",
    )(queries.reshape(whole), keys, values, out_grad.reshape(whole), doc_ids.reshape(1, tok))
    att, qg, kg, vg = pl.pallas_call(
        settle,
        out_shape=(flat, flat, narrow, narrow),
        in_specs=[anywhere] * 4,
        out_specs=(anywhere,) * 4,
        scratch_shapes=[dma((10,))],
        compiler_params=pltpu.CompilerParams(vmem_limit_bytes=LIMIT),
        name="settle",
    )(*results)
    return (att.reshape(queries.shape), qg.reshape(queries.shape), kg, vg)


def solution(mesh):
    wide, thin = P("seq", "head", None), P("seq", "head")
    return jax.shard_map(
        functools.partial(on_device, mesh.shape["seq"], mesh.shape["head"]),
        mesh=mesh, in_specs=(wide, thin, thin, wide, P("seq")),
        out_specs=(wide, wide, thin, thin), check_vma=False)
```

```python
import functools
import math

import jax
import jax.numpy as jnp
from jax import lax
from jax.experimental import pallas as pl
from jax.experimental.pallas import tpu as pltpu
from jax.sharding import PartitionSpec as P

HD = 128
REACH = 3
LIMIT = 32 * 2**20
MESH = pl.DeviceIdType.MESH


def partner(index, bits):
    out = index
    place = 1
    while place <= bits:
        if bits & place:
            out = out + place * (1 - 2 * ((index // place) % 2))
        place *= 2
    return out


def kernel(
    n_seq, n_head, reps,
    q_ref, k_ref, v_ref, g_ref, doc_ref,
    att_ref, qg_ref, kg_ref, vg_ref,
    qbuf, gbuf, kwin, vwin, kt, vt, docwin, bias, attbuf, qgbuf, kacc, vacc,
    kg_out, vg_out, kg_in, vg_in,
    halo_send, halo_recv, in_send, in_recv, ret_send, ret_recv, grad_send, grad_recv, local_sem,
):
    seq, head = lax.axis_index("seq"), lax.axis_index("head")
    tok, cols = k_ref.shape
    rows = tok * reps
    groups = cols // HD
    steps = range(1, REACH + 1)
    peers = range(1, n_head)

    def block(b):
        return pl.ds(b * tok, tok)

    def lanes(g):
        return pl.ds(g * HD, HD)

    def columns(ref, owner, g):
        at = pl.ds(pl.multiple_of(owner * cols + g * HD, HD), HD)
        return ref.at[:, at] if len(ref.shape) == 2 else ref.at[:, :, at]

    def matrix(ref, d, g):
        view = ref.at[d, g]
        return view if len(view.shape) == 2 else view.reshape(rows, HD)

    halo = {}
    for b in steps:
        pairs = [(doc_ref, docwin.at[b])]
        for g in range(groups):
            pairs.append((k_ref.at[:, lanes(g)], kwin.at[block(b), lanes(g)]))
            pairs.append((v_ref.at[:, lanes(g)], vwin.at[block(b), lanes(g)]))
        for i, (src, dst) in enumerate(pairs):
            halo[b, i] = pltpu.make_async_remote_copy(
                src_ref=src, dst_ref=dst, send_sem=halo_send.at[b - 1, i],
                recv_sem=halo_recv.at[b - 1, i], device_id=(seq + b, head), device_id_type=MESH)
    halos = 1 + 2 * groups
    inward = {}
    outward = {}
    for d in peers:
        other = partner(head, d)
        for g in range(groups):
            for i, (src, dst) in enumerate(((q_ref, qbuf), (g_ref, gbuf))):
                inward[d, g, i] = pltpu.make_async_remote_copy(
                    src_ref=columns(src, other, g), dst_ref=dst.at[d, g],
                    send_sem=in_send.at[d - 1, g, i], recv_sem=in_recv.at[d - 1, g, i],
                    device_id=(seq, other), device_id_type=MESH)
            for i, (src, dst) in enumerate(((attbuf, att_ref), (qgbuf, qg_ref))):
                outward[d, g, i] = pltpu.make_async_remote_copy(
                    src_ref=src.at[d, g], dst_ref=columns(dst, head, g),
                    send_sem=ret_send.at[d - 1, g, i], recv_sem=ret_recv.at[d - 1, g, i],
                    device_id=(seq, other), device_id_type=MESH)
    back = {}
    for b in steps:
        for g in range(groups):
            for i, (src, dst) in enumerate(((vg_out, vg_in), (kg_out, kg_in))):
                back[b, g, i] = pltpu.make_async_remote_copy(
                    src_ref=src.at[b - 1, :, lanes(g)], dst_ref=dst.at[b - 1, :, lanes(g)],
                    send_sem=grad_send.at[b - 1, g, i], recv_sem=grad_recv.at[b - 1, g, i],
                    device_id=(seq - b, head), device_id_type=MESH)

    barrier = pltpu.get_barrier_semaphore()
    for d in peers:
        pl.semaphore_signal(barrier, 1, device_id=(seq, partner(head, d)), device_id_type=MESH)
    count = n_head - 1
    for b in steps:
        @pl.when(seq + b < n_seq)
        def _():
            pl.semaphore_signal(barrier, 1, device_id=(seq + b, head), device_id_type=MESH)

        @pl.when(seq >= b)
        def _():
            pl.semaphore_signal(barrier, 1, device_id=(seq - b, head), device_id_type=MESH)
        count = count + jnp.where(seq + b < n_seq, 1, 0) + jnp.where(seq >= b, 1, 0)

    own = [
        pltpu.make_async_copy(src, dst, local_sem.at[i])
        for i, (src, dst) in enumerate(
            [(k_ref, kwin.at[block(0)]), (v_ref, vwin.at[block(0)]), (doc_ref, docwin.at[0])]
            + [(columns(q_ref, head, g), qbuf.at[0, g]) for g in range(groups)]
            + [(columns(g_ref, head, g), gbuf.at[0, g]) for g in range(groups)])
    ]
    for copy in own:
        copy.start()
    pl.semaphore_wait(barrier, count)

    for g in range(groups):
        for b in reversed(steps):
            @pl.when(seq + b < n_seq)
            def _():
                for i in ((0, 1, 2) if g == 0 else (1 + 2 * g, 2 + 2 * g)):
                    halo[b, i].start()
        for d in reversed(peers):
            for i in range(2):
                inward[d, g, i].start()

    for b in steps:
        @pl.when(seq < b)
        def _():
            kwin[block(b), :] = jnp.zeros((tok, cols), kwin.dtype)
            vwin[block(b), :] = jnp.zeros((tok, cols), vwin.dtype)
            docwin[b] = jnp.full((1, tok), -1, jnp.int32)

    key_of = lax.broadcasted_iota(jnp.int32, (tok, rows), 0)
    token_of = lax.broadcasted_iota(jnp.int32, (tok, rows), 1) // reps
    near = key_of <= token_of
    for copy in own:
        copy.wait()
    for b in steps:
        @pl.when(seq >= b)
        def _():
            halo[b, 0].wait_recv()

    doc_own = docwin[0].astype(jnp.float32)
    if reps == 1:
        doc_q = doc_own
    else:
        spread = (key_of == token_of).astype(jnp.bfloat16)
        doc_q = jnp.dot(jnp.broadcast_to(doc_own, (16, tok)).astype(jnp.bfloat16), spread,
                        preferred_element_type=jnp.float32)[0:1]

    def same(b):
        doc = jnp.transpose(jnp.broadcast_to(docwin[b].astype(jnp.float32), (tok, tok)))
        return jnp.where(doc[:, 0:1] == doc_q, 0.0, -1e30)

    bias[block(0), :] = jnp.where(near, same(0), same(REACH))
    for b in range(1, REACH):
        bias[block(b), :] = same(b)

    scale = 1.0 / math.sqrt(HD)
    last = REACH * tok

    def folded(x):
        return jnp.concatenate([jnp.where(near, x[:tok], x[last:]), x[tok:last]], axis=0)

    def unfolded(x):
        zero = jnp.zeros((tok, rows), x.dtype)
        return jnp.concatenate(
            [jnp.where(near, x[:tok], zero), x[tok:], jnp.where(near, zero, x[:tok])], axis=0)

    def tile(d, g):
        q = matrix(qbuf, d, g)[...]
        grad = matrix(gbuf, d, g)[...]
        by_last = (((1,), (1,)), ((), ()))
        s = folded(lax.dot_general(kwin[:, lanes(g)], q, by_last, preferred_element_type=jnp.float32))
        s = s + bias[...]
        top = jnp.max(s, axis=0, keepdims=True)
        e = jnp.exp2((s - top) * (scale * math.log2(math.e)))
        p = e * (1.0 / jnp.sum(e, axis=0, keepdims=True))
        dp = folded(lax.dot_general(vwin[:, lanes(g)], grad, by_last, preferred_element_type=jnp.float32))
        delta = jnp.sum(p * dp, axis=0, keepdims=True)
        ds = unfolded(p * (dp - delta) * scale).astype(jnp.bfloat16)
        pb = unfolded(p).astype(jnp.bfloat16)
        att = jnp.dot(vt[g], pb, preferred_element_type=jnp.float32)
        matrix(attbuf, d, g)[...] = jnp.transpose(att).astype(jnp.bfloat16)
        qg = jnp.dot(kt[g], ds, preferred_element_type=jnp.float32)
        matrix(qgbuf, d, g)[...] = jnp.transpose(qg).astype(jnp.bfloat16)
        dv = jnp.dot(pb, grad, preferred_element_type=jnp.float32)
        dk = jnp.dot(ds, q, preferred_element_type=jnp.float32)
        if d == 0:
            vacc[:, lanes(g)] = dv
            kacc[:, lanes(g)] = dk
        else:
            vacc[:, lanes(g)] += dv
            kacc[:, lanes(g)] += dk

    done = [pltpu.make_async_copy(src.at[0, g], columns(dst, head, g), local_sem.at[2 * g + i])
            for g in range(groups) for i, (src, dst) in enumerate(((attbuf, att_ref), (qgbuf, qg_ref)))]
    for g in range(groups):
        for b in steps:
            @pl.when(seq >= b)
            def _():
                halo[b, 1 + 2 * g].wait_recv()
                halo[b, 2 + 2 * g].wait_recv()
        kt[g] = jnp.transpose(kwin[:, lanes(g)])
        vt[g] = jnp.transpose(vwin[:, lanes(g)])
        for d in range(n_head):
            if d:
                inward[d, g, 0].wait_recv()
                inward[d, g, 1].wait_recv()
            tile(d, g)
            if d:
                outward[d, g, 0].start()
                outward[d, g, 1].start()
            else:
                done[2 * g].start()
                done[2 * g + 1].start()
        for b in reversed(steps):
            vg_out[b - 1, :, lanes(g)] = vacc[block(b), lanes(g)].astype(jnp.bfloat16)
            kg_out[b - 1, :, lanes(g)] = kacc[block(b), lanes(g)].astype(jnp.bfloat16)

            @pl.when(seq >= b)
            def _():
                back[b, g, 0].start()
                back[b, g, 1].start()

    for b in steps:
        @pl.when(seq + b < n_seq)
        def _():
            for g in range(groups):
                for i in range(2):
                    back[b, g, i].wait_recv()
            vacc[block(0), :] += vg_in[b - 1].astype(jnp.float32)
            kacc[block(0), :] += kg_in[b - 1].astype(jnp.float32)
    vg_ref[...] = vacc[block(0), :].astype(vg_ref.dtype)
    kg_ref[...] = kacc[block(0), :].astype(kg_ref.dtype)

    for copy in done:
        copy.wait()
    for b in steps:
        @pl.when(seq + b < n_seq)
        def _():
            for i in range(halos):
                halo[b, i].wait_send()

        @pl.when(seq >= b)
        def _():
            for g in range(groups):
                for i in range(2):
                    back[b, g, i].wait_send()
    for d in peers:
        for g in range(groups):
            for i in range(2):
                inward[d, g, i].wait_send()
                outward[d, g, i].wait_send()
                outward[d, g, i].wait_recv()


def settle(*refs):
    sources, places, sem = refs[:4], refs[4:8], refs[8]
    copies = []
    for src, dst in zip(sources, places):
        parts = 4 if len(copies) < 8 else 1
        size = src.shape[0] // parts
        for part in range(parts):
            at = pl.ds(part * size, size)
            copies.append(pltpu.make_async_copy(src.at[at], dst.at[at], sem.at[len(copies)]))
    for copy in copies:
        copy.start()
    for copy in copies:
        copy.wait()


def on_device(n_seq, n_head, queries, keys, values, out_grad, doc_ids):
    tok, reps, width = queries.shape
    cols = keys.shape[1]
    groups = cols // HD
    rows = tok * reps
    span = (REACH + 1) * tok
    whole = (tok, reps, width) if reps > 1 else (tok, width)
    piece = whole[:-1] + (HD,)
    bf16, f32 = jnp.bfloat16, jnp.float32
    dma = pltpu.SemaphoreType.DMA
    anywhere = pl.BlockSpec(memory_space=pl.ANY)
    vmem = pl.BlockSpec(memory_space=pltpu.VMEM)
    flat = jax.ShapeDtypeStruct(whole, bf16)
    narrow = jax.ShapeDtypeStruct((tok, cols), bf16)
    results = pl.pallas_call(
        functools.partial(kernel, n_seq, n_head, reps),
        out_shape=(flat, flat, narrow, narrow),
        in_specs=[anywhere] * 5,
        out_specs=(anywhere, anywhere, vmem, vmem),
        scratch_shapes=[
            pltpu.VMEM((n_head, groups) + piece, bf16),
            pltpu.VMEM((n_head, groups) + piece, bf16),
            pltpu.VMEM((span, cols), bf16),
            pltpu.VMEM((span, cols), bf16),
            pltpu.VMEM((groups, HD, span), bf16),
            pltpu.VMEM((groups, HD, span), bf16),
            pltpu.VMEM((REACH + 1, 1, tok), jnp.int32),
            pltpu.VMEM((REACH * tok, rows), f32),
            pltpu.VMEM((n_head, groups) + piece, bf16),
            pltpu.VMEM((n_head, groups) + piece, bf16),
            pltpu.VMEM((span, cols), f32),
            pltpu.VMEM((span, cols), f32),
            pltpu.VMEM((REACH, tok, cols), bf16),
            pltpu.VMEM((REACH, tok, cols), bf16),
            pltpu.VMEM((REACH, tok, cols), bf16),
            pltpu.VMEM((REACH, tok, cols), bf16),
            dma((REACH, 1 + 2 * groups)), dma((REACH, 1 + 2 * groups)),
            dma((n_head - 1, groups, 2)), dma((n_head - 1, groups, 2)),
            dma((n_head - 1, groups, 2)), dma((n_head - 1, groups, 2)),
            dma((REACH, groups, 2)), dma((REACH, groups, 2)),
            dma((3 + 2 * groups,)),
        ],
        compiler_params=pltpu.CompilerParams(
            collective_id=0, has_side_effects=True, vmem_limit_bytes=LIMIT),
        cost_estimate=pl.CostEstimate(
            flops=12 * n_head * groups * rows * span * HD,
            bytes_accessed=8 * rows * width + 8 * tok * cols,
            transcendentals=n_head * groups * rows * REACH * tok),
        name="attention_layer",
    )(queries.reshape(whole), keys, values, out_grad.reshape(whole), doc_ids.reshape(1, tok))
    att, qg, kg, vg = pl.pallas_call(
        settle,
        out_shape=(flat, flat, narrow, narrow),
        in_specs=[anywhere] * 4,
        out_specs=(anywhere,) * 4,
        scratch_shapes=[dma((10,))],
        compiler_params=pltpu.CompilerParams(vmem_limit_bytes=LIMIT),
        name="settle",
    )(*results)
    return (att.reshape(queries.shape), qg.reshape(queries.shape), kg, vg)


def solution(mesh):
    wide, thin = P("seq", "head", None), P("seq", "head")
    return jax.shard_map(
        functools.partial(on_device, mesh.shape["seq"], mesh.shape["head"]),
        mesh=mesh, in_specs=(wide, thin, thin, wide, P("seq")),
        out_specs=(wide, wide, thin, thin), check_vma=False)
```

```python
import functools
import math

import jax
import jax.numpy as jnp
from jax import lax
from jax.experimental import pallas as pl
from jax.experimental.pallas import tpu as pltpu
from jax.sharding import PartitionSpec as P

HD = 128
REACH = 3
LIMIT = 60 * 2**20
MESH = pl.DeviceIdType.MESH


def partner(index, bits):
    out = index
    place = 1
    while place <= bits:
        if bits & place:
            out = out + place * (1 - 2 * ((index // place) % 2))
        place *= 2
    return out


def kernel(
    n_seq, n_head, reps,
    q_ref, k_ref, v_ref, g_ref, doc_ref,
    att_ref, qg_ref, kg_ref, vg_ref,
    qbuf, gbuf, kwin, vwin, kt, vt, docwin, bias, attbuf, qgbuf, kacc, vacc,
    kg_out, vg_out, kg_in, vg_in, qall, gall,
    halo_send, halo_recv, in_send, in_recv, ret_send, ret_recv, grad_send, grad_recv, local_sem, own_sem,
):
    seq, head = lax.axis_index("seq"), lax.axis_index("head")
    tok, cols = k_ref.shape
    rows = tok * reps
    groups = cols // HD
    steps = range(1, REACH + 1)
    peers = range(1, n_head)

    def block(b):
        return pl.ds(b * tok, tok)

    def lanes(g):
        return pl.ds(g * HD, HD)

    def columns(ref, owner, g):
        at = pl.ds(pl.multiple_of(owner * cols + g * HD, HD), HD)
        return ref.at[:, at] if len(ref.shape) == 2 else ref.at[:, :, at]

    def matrix(ref, d, g):
        view = ref.at[d, g]
        return view if len(view.shape) == 2 else view.reshape(rows, HD)

    halo = {}
    for b in steps:
        pairs = [(docwin.at[0], docwin.at[b])]
        for g in range(groups):
            pairs.append((kwin.at[block(0), lanes(g)], kwin.at[block(b), lanes(g)]))
            pairs.append((vwin.at[block(0), lanes(g)], vwin.at[block(b), lanes(g)]))
        for i, (src, dst) in enumerate(pairs):
            halo[b, i] = pltpu.make_async_remote_copy(
                src_ref=src, dst_ref=dst, send_sem=halo_send.at[b - 1, i],
                recv_sem=halo_recv.at[b - 1, i], device_id=(seq + b, head), device_id_type=MESH)
    halos = 1 + 2 * groups
    inward = {}
    outward = {}
    for d in peers:
        other = partner(head, d)
        for g in range(groups):
            for i, (src, dst) in enumerate(((qall, qbuf), (gall, gbuf))):
                inward[d, g, i] = pltpu.make_async_remote_copy(
                    src_ref=columns(src, other, g), dst_ref=dst.at[d, g],
                    send_sem=in_send.at[d - 1, g, i], recv_sem=in_recv.at[d - 1, g, i],
                    device_id=(seq, other), device_id_type=MESH)
            for i, (src, dst) in enumerate(((attbuf, att_ref), (qgbuf, qg_ref))):
                outward[d, g, i] = pltpu.make_async_remote_copy(
                    src_ref=src.at[d, g], dst_ref=columns(dst, head, g),
                    send_sem=ret_send.at[d - 1, g, i], recv_sem=ret_recv.at[d - 1, g, i],
                    device_id=(seq, other), device_id_type=MESH)
    back = {}
    for b in steps:
        for g in range(groups):
            for i, (src, dst) in enumerate(((vg_out, vg_in), (kg_out, kg_in))):
                back[b, g, i] = pltpu.make_async_remote_copy(
                    src_ref=src.at[b - 1, :, lanes(g)], dst_ref=dst.at[b - 1, :, lanes(g)],
                    send_sem=grad_send.at[b - 1, g, i], recv_sem=grad_recv.at[b - 1, g, i],
                    device_id=(seq - b, head), device_id_type=MESH)

    barrier = pltpu.get_barrier_semaphore()
    for d in peers:
        pl.semaphore_signal(barrier, 1, device_id=(seq, partner(head, d)), device_id_type=MESH)
    count = n_head - 1
    for b in steps:
        @pl.when(seq + b < n_seq)
        def _():
            pl.semaphore_signal(barrier, 1, device_id=(seq + b, head), device_id_type=MESH)

        @pl.when(seq >= b)
        def _():
            pl.semaphore_signal(barrier, 1, device_id=(seq - b, head), device_id_type=MESH)
        count = count + jnp.where(seq + b < n_seq, 1, 0) + jnp.where(seq >= b, 1, 0)

    own = [
        pltpu.make_async_copy(src, dst, local_sem.at[i])
        for i, (src, dst) in enumerate((
            (doc_ref, docwin.at[0]), (k_ref, kwin.at[block(0)]), (v_ref, vwin.at[block(0)]),
            (q_ref, qall), (g_ref, gall)))
    ]
    mine = [
        pltpu.make_async_copy(columns(src, head, g), dst.at[0, g], own_sem.at[g, i])
        for g in range(groups) for i, (src, dst) in enumerate(((qall, qbuf), (gall, gbuf)))
    ]
    for copy in own:
        copy.start()
    for copy in own:
        copy.wait()
    for copy in mine:
        copy.start()
    pl.semaphore_wait(barrier, count)

    for g in range(groups):
        for b in reversed(steps):
            @pl.when(seq + b < n_seq)
            def _():
                for i in ((0, 1, 2) if g == 0 else (1 + 2 * g, 2 + 2 * g)):
                    halo[b, i].start()
        for d in reversed(peers):
            for i in range(2):
                inward[d, g, i].start()

    for b in steps:
        @pl.when(seq < b)
        def _():
            kwin[block(b), :] = jnp.zeros((tok, cols), kwin.dtype)
            vwin[block(b), :] = jnp.zeros((tok, cols), vwin.dtype)
            docwin[b] = jnp.full((1, tok), -1, jnp.int32)

    key_of = lax.broadcasted_iota(jnp.int32, (tok, rows), 0)
    token_of = lax.broadcasted_iota(jnp.int32, (tok, rows), 1) // reps
    near = key_of <= token_of
    for copy in mine:
        copy.wait()
    for b in steps:
        @pl.when(seq >= b)
        def _():
            halo[b, 0].wait_recv()

    doc_own = docwin[0].astype(jnp.float32)
    if reps == 1:
        doc_q = doc_own
    else:
        spread = (key_of == token_of).astype(jnp.bfloat16)
        doc_q = jnp.dot(jnp.broadcast_to(doc_own, (16, tok)).astype(jnp.bfloat16), spread,
                        preferred_element_type=jnp.float32)[0:1]

    def same(b):
        doc = jnp.transpose(jnp.broadcast_to(docwin[b].astype(jnp.float32), (tok, tok)))
        return jnp.where(doc[:, 0:1] == doc_q, 0.0, -1e30)

    bias[block(0), :] = jnp.where(near, same(0), same(REACH))
    for b in range(1, REACH):
        bias[block(b), :] = same(b)

    scale = 1.0 / math.sqrt(HD)
    last = REACH * tok

    def folded(x):
        return jnp.concatenate([jnp.where(near, x[:tok], x[last:]), x[tok:last]], axis=0)

    def unfolded(x):
        zero = jnp.zeros((tok, rows), x.dtype)
        return jnp.concatenate(
            [jnp.where(near, x[:tok], zero), x[tok:], jnp.where(near, zero, x[:tok])], axis=0)

    def tile(d, g):
        q = matrix(qbuf, d, g)[...]
        grad = matrix(gbuf, d, g)[...]
        by_last = (((1,), (1,)), ((), ()))
        s = folded(lax.dot_general(kwin[:, lanes(g)], q, by_last, preferred_element_type=jnp.float32))
        s = s + bias[...]
        top = jnp.max(s, axis=0, keepdims=True)
        e = jnp.exp2((s - top) * (scale * math.log2(math.e)))
        p = e * (1.0 / jnp.sum(e, axis=0, keepdims=True))
        dp = folded(lax.dot_general(vwin[:, lanes(g)], grad, by_last, preferred_element_type=jnp.float32))
        delta = jnp.sum(p * dp, axis=0, keepdims=True)
        ds = unfolded(p * (dp - delta) * scale).astype(jnp.bfloat16)
        pb = unfolded(p).astype(jnp.bfloat16)
        att = jnp.dot(vt[g], pb, preferred_element_type=jnp.float32)
        matrix(attbuf, d, g)[...] = jnp.transpose(att).astype(jnp.bfloat16)
        qg = jnp.dot(kt[g], ds, preferred_element_type=jnp.float32)
        matrix(qgbuf, d, g)[...] = jnp.transpose(qg).astype(jnp.bfloat16)
        dv = jnp.dot(pb, grad, preferred_element_type=jnp.float32)
        dk = jnp.dot(ds, q, preferred_element_type=jnp.float32)
        if d == 0:
            vacc[:, lanes(g)] = dv
            kacc[:, lanes(g)] = dk
        else:
            vacc[:, lanes(g)] += dv
            kacc[:, lanes(g)] += dk

    done = [pltpu.make_async_copy(src.at[0, g], columns(dst, head, g), own_sem.at[g, i])
            for g in range(groups) for i, (src, dst) in enumerate(((attbuf, att_ref), (qgbuf, qg_ref)))]
    for g in range(groups):
        for b in steps:
            @pl.when(seq >= b)
            def _():
                halo[b, 1 + 2 * g].wait_recv()
                halo[b, 2 + 2 * g].wait_recv()
        kt[g] = jnp.transpose(kwin[:, lanes(g)])
        vt[g] = jnp.transpose(vwin[:, lanes(g)])
        for d in range(n_head):
            if d:
                inward[d, g, 0].wait_recv()
                inward[d, g, 1].wait_recv()
            tile(d, g)
            if d:
                outward[d, g, 0].start()
                outward[d, g, 1].start()
            else:
                done[2 * g].start()
                done[2 * g + 1].start()
        for b in reversed(steps):
            vg_out[b - 1, :, lanes(g)] = vacc[block(b), lanes(g)].astype(jnp.bfloat16)
            kg_out[b - 1, :, lanes(g)] = kacc[block(b), lanes(g)].astype(jnp.bfloat16)

            @pl.when(seq >= b)
            def _():
                back[b, g, 0].start()
                back[b, g, 1].start()

    for b in steps:
        @pl.when(seq + b < n_seq)
        def _():
            for g in range(groups):
                for i in range(2):
                    back[b, g, i].wait_recv()
            vacc[block(0), :] += vg_in[b - 1].astype(jnp.float32)
            kacc[block(0), :] += kg_in[b - 1].astype(jnp.float32)
    vg_ref[...] = vacc[block(0), :].astype(vg_ref.dtype)
    kg_ref[...] = kacc[block(0), :].astype(kg_ref.dtype)

    for copy in done:
        copy.wait()
    for b in steps:
        @pl.when(seq + b < n_seq)
        def _():
            for i in range(halos):
                halo[b, i].wait_send()

        @pl.when(seq >= b)
        def _():
            for g in range(groups):
                for i in range(2):
                    back[b, g, i].wait_send()
    for d in peers:
        for g in range(groups):
            for i in range(2):
                inward[d, g, i].wait_send()
                outward[d, g, i].wait_send()
                outward[d, g, i].wait_recv()


def settle(*refs):
    sources, places, held, sem = refs[:4], refs[4:8], refs[8:12], refs[12]
    copies = []
    for src, dst, mid in zip(sources, places, held):
        parts = 2
        size = src.shape[0] // parts
        for part in range(parts):
            at = pl.ds(part * size, size)
            copies.append((pltpu.make_async_copy(src.at[at], mid.at[at], sem.at[0, len(copies)]),
                           pltpu.make_async_copy(mid.at[at], dst.at[at], sem.at[1, len(copies)])))
    for into, _ in copies:
        into.start()
    for into, out in copies:
        into.wait()
        out.start()
    for _, out in copies:
        out.wait()


def on_device(n_seq, n_head, queries, keys, values, out_grad, doc_ids):
    tok, reps, width = queries.shape
    cols = keys.shape[1]
    groups = cols // HD
    rows = tok * reps
    span = (REACH + 1) * tok
    whole = (tok, reps, width) if reps > 1 else (tok, width)
    piece = whole[:-1] + (HD,)
    bf16, f32 = jnp.bfloat16, jnp.float32
    dma = pltpu.SemaphoreType.DMA
    anywhere = pl.BlockSpec(memory_space=pl.ANY)
    vmem = pl.BlockSpec(memory_space=pltpu.VMEM)
    flat = jax.ShapeDtypeStruct(whole, bf16)
    narrow = jax.ShapeDtypeStruct((tok, cols), bf16)
    results = pl.pallas_call(
        functools.partial(kernel, n_seq, n_head, reps),
        out_shape=(flat, flat, narrow, narrow),
        in_specs=[anywhere] * 5,
        out_specs=(anywhere, anywhere, vmem, vmem),
        scratch_shapes=[
            pltpu.VMEM((n_head, groups) + piece, bf16),
            pltpu.VMEM((n_head, groups) + piece, bf16),
            pltpu.VMEM((span, cols), bf16),
            pltpu.VMEM((span, cols), bf16),
            pltpu.VMEM((groups, HD, span), bf16),
            pltpu.VMEM((groups, HD, span), bf16),
            pltpu.VMEM((REACH + 1, 1, tok), jnp.int32),
            pltpu.VMEM((REACH * tok, rows), f32),
            pltpu.VMEM((n_head, groups) + piece, bf16),
            pltpu.VMEM((n_head, groups) + piece, bf16),
            pltpu.VMEM((span, cols), f32),
            pltpu.VMEM((span, cols), f32),
            pltpu.VMEM((REACH, tok, cols), bf16),
            pltpu.VMEM((REACH, tok, cols), bf16),
            pltpu.VMEM((REACH, tok, cols), bf16),
            pltpu.VMEM((REACH, tok, cols), bf16),
            pltpu.VMEM(whole, bf16),
            pltpu.VMEM(whole, bf16),
            dma((REACH, 1 + 2 * groups)), dma((REACH, 1 + 2 * groups)),
            dma((n_head - 1, groups, 2)), dma((n_head - 1, groups, 2)),
            dma((n_head - 1, groups, 2)), dma((n_head - 1, groups, 2)),
            dma((REACH, groups, 2)), dma((REACH, groups, 2)),
            dma((5,)), dma((groups, 2)),
        ],
        compiler_params=pltpu.CompilerParams(
            collective_id=0, has_side_effects=True, vmem_limit_bytes=LIMIT),
        cost_estimate=pl.CostEstimate(
            flops=12 * n_head * groups * rows * span * HD,
            bytes_accessed=8 * rows * width + 8 * tok * cols,
            transcendentals=n_head * groups * rows * REACH * tok),
        name="attention_layer",
    )(queries.reshape(whole), keys, values, out_grad.reshape(whole), doc_ids.reshape(1, tok))
    att, qg, kg, vg = pl.pallas_call(
        settle,
        out_shape=(flat, flat, narrow, narrow),
        in_specs=[anywhere] * 4,
        out_specs=(anywhere,) * 4,
        scratch_shapes=[pltpu.VMEM(x.shape, x.dtype) for x in results] + [dma((2, 8))],
        compiler_params=pltpu.CompilerParams(vmem_limit_bytes=LIMIT),
        name="settle",
    )(*results)
    return (att.reshape(queries.shape), qg.reshape(queries.shape), kg, vg)


def solution(mesh):
    wide, thin = P("seq", "head", None), P("seq", "head")
    return jax.shard_map(
        functools.partial(on_device, mesh.shape["seq"], mesh.shape["head"]),
        mesh=mesh, in_specs=(wide, thin, thin, wide, P("seq")),
        out_specs=(wide, wide, thin, thin), check_vma=False)
```

```python
import functools
import math

import jax
import jax.numpy as jnp
from jax import lax
from jax.experimental import pallas as pl
from jax.experimental.pallas import tpu as pltpu
from jax.sharding import PartitionSpec as P

HD = 128
REACH = 3
LIMIT = 60 * 2**20
MESH = pl.DeviceIdType.MESH


def partner(index, bits):
    out = index
    place = 1
    while place <= bits:
        if bits & place:
            out = out + place * (1 - 2 * ((index // place) % 2))
        place *= 2
    return out


def kernel(
    n_seq, n_head, reps,
    q_ref, k_ref, v_ref, g_ref, doc_ref,
    att_ref, qg_ref, kg_ref, vg_ref,
    qbuf, gbuf, kwin, vwin, kt, vt, docwin, bias, attbuf, qgbuf, kacc, vacc,
    kg_out, vg_out, kg_in, vg_in, qall, gall,
    halo_send, halo_recv, in_send, in_recv, ret_send, ret_recv, grad_send, grad_recv, local_sem, own_sem,
):
    seq, head = lax.axis_index("seq"), lax.axis_index("head")
    tok, cols = k_ref.shape
    rows = tok * reps
    groups = cols // HD
    steps = range(1, REACH + 1)
    peers = range(1, n_head)

    def block(b):
        return pl.ds(b * tok, tok)

    def lanes(g):
        return pl.ds(g * HD, HD)

    def columns(ref, owner, g):
        at = pl.ds(pl.multiple_of(owner * cols + g * HD, HD), HD)
        return ref.at[:, at] if len(ref.shape) == 2 else ref.at[:, :, at]

    def matrix(ref, d, g):
        view = ref.at[d, g]
        return view if len(view.shape) == 2 else view.reshape(rows, HD)

    halo = {}
    for b in steps:
        pairs = [(docwin.at[0], docwin.at[b])]
        for g in range(groups):
            pairs.append((kwin.at[block(0), lanes(g)], kwin.at[block(b), lanes(g)]))
            pairs.append((vwin.at[block(0), lanes(g)], vwin.at[block(b), lanes(g)]))
        for i, (src, dst) in enumerate(pairs):
            halo[b, i] = pltpu.make_async_remote_copy(
                src_ref=src, dst_ref=dst, send_sem=halo_send.at[b - 1, i],
                recv_sem=halo_recv.at[b - 1, i], device_id=(seq + b, head), device_id_type=MESH)
    halos = 1 + 2 * groups
    inward = {}
    outward = {}
    for d in peers:
        other = partner(head, d)
        for g in range(groups):
            for i, (src, dst) in enumerate(((qall, qbuf), (gall, gbuf))):
                inward[d, g, i] = pltpu.make_async_remote_copy(
                    src_ref=columns(src, other, g), dst_ref=dst.at[d, g],
                    send_sem=in_send.at[d - 1, g, i], recv_sem=in_recv.at[d - 1, g, i],
                    device_id=(seq, other), device_id_type=MESH)
            for i, (src, dst) in enumerate(((attbuf, att_ref), (qgbuf, qg_ref))):
                outward[d, g, i] = pltpu.make_async_remote_copy(
                    src_ref=src.at[d, g], dst_ref=columns(dst, head, g),
                    send_sem=ret_send.at[d - 1, g, i], recv_sem=ret_recv.at[d - 1, g, i],
                    device_id=(seq, other), device_id_type=MESH)
    back = {}
    for b in steps:
        for g in range(groups):
            for i, (src, dst) in enumerate(((vg_out, vg_in), (kg_out, kg_in))):
                back[b, g, i] = pltpu.make_async_remote_copy(
                    src_ref=src.at[b - 1, :, lanes(g)], dst_ref=dst.at[b - 1, :, lanes(g)],
                    send_sem=grad_send.at[b - 1, g, i], recv_sem=grad_recv.at[b - 1, g, i],
                    device_id=(seq - b, head), device_id_type=MESH)

    barrier = pltpu.get_barrier_semaphore()
    for d in peers:
        pl.semaphore_signal(barrier, 1, device_id=(seq, partner(head, d)), device_id_type=MESH)
    count = n_head - 1
    for b in steps:
        @pl.when(seq + b < n_seq)
        def _():
            pl.semaphore_signal(barrier, 1, device_id=(seq + b, head), device_id_type=MESH)

        @pl.when(seq >= b)
        def _():
            pl.semaphore_signal(barrier, 1, device_id=(seq - b, head), device_id_type=MESH)
        count = count + jnp.where(seq + b < n_seq, 1, 0) + jnp.where(seq >= b, 1, 0)

    own = [
        pltpu.make_async_copy(src, dst, local_sem.at[i])
        for i, (src, dst) in enumerate((
            (doc_ref, docwin.at[0]), (k_ref, kwin.at[block(0)]), (v_ref, vwin.at[block(0)]),
            (q_ref, qall), (g_ref, gall)))
    ]
    mine = [
        pltpu.make_async_copy(columns(src, head, g), dst.at[0, g], own_sem.at[g, i])
        for g in range(groups) for i, (src, dst) in enumerate(((qall, qbuf), (gall, gbuf)))
    ]
    for copy in own:
        copy.start()
    for copy in own:
        copy.wait()
    for copy in mine:
        copy.start()
    pl.semaphore_wait(barrier, count)

    far = [d for d in peers if d > 1]
    for g in range(groups):
        for d in far:
            for i in range(2):
                inward[d, g, i].start()
        for b in reversed(steps):
            @pl.when(seq + b < n_seq)
            def _():
                for i in ((0, 1, 2) if g == 0 else (1 + 2 * g, 2 + 2 * g)):
                    halo[b, i].start()
        for i in range(2):
            inward[1, g, i].start()

    for b in steps:
        @pl.when(seq < b)
        def _():
            kwin[block(b), :] = jnp.zeros((tok, cols), kwin.dtype)
            vwin[block(b), :] = jnp.zeros((tok, cols), vwin.dtype)
            docwin[b] = jnp.full((1, tok), -1, jnp.int32)

    key_of = lax.broadcasted_iota(jnp.int32, (tok, rows), 0)
    token_of = lax.broadcasted_iota(jnp.int32, (tok, rows), 1) // reps
    near = key_of <= token_of
    for copy in mine:
        copy.wait()
    for b in steps:
        @pl.when(seq >= b)
        def _():
            halo[b, 0].wait_recv()

    doc_own = docwin[0].astype(jnp.float32)
    if reps == 1:
        doc_q = doc_own
    else:
        spread = (key_of == token_of).astype(jnp.bfloat16)
        doc_q = jnp.dot(jnp.broadcast_to(doc_own, (16, tok)).astype(jnp.bfloat16), spread,
                        preferred_element_type=jnp.float32)[0:1]

    def same(b):
        doc = jnp.transpose(jnp.broadcast_to(docwin[b].astype(jnp.float32), (tok, tok)))
        return jnp.where(doc[:, 0:1] == doc_q, 0.0, -1e30)

    bias[block(0), :] = jnp.where(near, same(0), same(REACH))
    for b in range(1, REACH):
        bias[block(b), :] = same(b)

    scale = 1.0 / math.sqrt(HD)
    last = REACH * tok

    def folded(x):
        return jnp.concatenate([jnp.where(near, x[:tok], x[last:]), x[tok:last]], axis=0)

    def unfolded(x):
        zero = jnp.zeros((tok, rows), x.dtype)
        return jnp.concatenate(
            [jnp.where(near, x[:tok], zero), x[tok:], jnp.where(near, zero, x[:tok])], axis=0)

    def tile(d, g):
        q = matrix(qbuf, d, g)[...]
        grad = matrix(gbuf, d, g)[...]
        by_last = (((1,), (1,)), ((), ()))
        s = folded(lax.dot_general(kwin[:, lanes(g)], q, by_last, preferred_element_type=jnp.float32))
        s = s + bias[...]
        top = jnp.max(s, axis=0, keepdims=True)
        e = jnp.exp2((s - top) * (scale * math.log2(math.e)))
        p = e * (1.0 / jnp.sum(e, axis=0, keepdims=True))
        dp = folded(lax.dot_general(vwin[:, lanes(g)], grad, by_last, preferred_element_type=jnp.float32))
        delta = jnp.sum(p * dp, axis=0, keepdims=True)
        ds = unfolded(p * (dp - delta) * scale).astype(jnp.bfloat16)
        pb = unfolded(p).astype(jnp.bfloat16)
        att = jnp.dot(vt[g], pb, preferred_element_type=jnp.float32)
        matrix(attbuf, d, g)[...] = jnp.transpose(att).astype(jnp.bfloat16)
        qg = jnp.dot(kt[g], ds, preferred_element_type=jnp.float32)
        matrix(qgbuf, d, g)[...] = jnp.transpose(qg).astype(jnp.bfloat16)
        dv = jnp.dot(pb, grad, preferred_element_type=jnp.float32)
        dk = jnp.dot(ds, q, preferred_element_type=jnp.float32)
        if d == 0:
            vacc[:, lanes(g)] = dv
            kacc[:, lanes(g)] = dk
        else:
            vacc[:, lanes(g)] += dv
            kacc[:, lanes(g)] += dk

    done = [pltpu.make_async_copy(src.at[0, g], columns(dst, head, g), own_sem.at[g, i])
            for g in range(groups) for i, (src, dst) in enumerate(((attbuf, att_ref), (qgbuf, qg_ref)))]
    held_back = []
    for g in range(groups):
        for b in steps:
            @pl.when(seq >= b)
            def _():
                halo[b, 1 + 2 * g].wait_recv()
                halo[b, 2 + 2 * g].wait_recv()
        kt[g] = jnp.transpose(kwin[:, lanes(g)])
        vt[g] = jnp.transpose(vwin[:, lanes(g)])
        for d in range(n_head):
            if d == 2 and g == groups - 1:
                for copy in (inward[e, h, i] for e in far for h in range(groups) for i in range(2)):
                    copy.wait_send()
                for copy in held_back:
                    copy.start()
            if d:
                inward[d, g, 0].wait_recv()
                inward[d, g, 1].wait_recv()
            tile(d, g)
            if d in far and g < groups - 1:
                held_back += [outward[d, g, 0], outward[d, g, 1]]
            elif d:
                outward[d, g, 0].start()
                outward[d, g, 1].start()
            else:
                done[2 * g].start()
                done[2 * g + 1].start()
        for b in reversed(steps):
            vg_out[b - 1, :, lanes(g)] = vacc[block(b), lanes(g)].astype(jnp.bfloat16)
            kg_out[b - 1, :, lanes(g)] = kacc[block(b), lanes(g)].astype(jnp.bfloat16)

            @pl.when(seq >= b)
            def _():
                back[b, g, 0].start()
                back[b, g, 1].start()

    for b in steps:
        @pl.when(seq + b < n_seq)
        def _():
            for g in range(groups):
                for i in range(2):
                    back[b, g, i].wait_recv()
            vacc[block(0), :] += vg_in[b - 1].astype(jnp.float32)
            kacc[block(0), :] += kg_in[b - 1].astype(jnp.float32)
    vg_ref[...] = vacc[block(0), :].astype(vg_ref.dtype)
    kg_ref[...] = kacc[block(0), :].astype(kg_ref.dtype)

    for copy in done:
        copy.wait()
    for b in steps:
        @pl.when(seq + b < n_seq)
        def _():
            for i in range(halos):
                halo[b, i].wait_send()

        @pl.when(seq >= b)
        def _():
            for g in range(groups):
                for i in range(2):
                    back[b, g, i].wait_send()
    for d in peers:
        for g in range(groups):
            for i in range(2):
                if d not in far:
                    inward[d, g, i].wait_send()
                outward[d, g, i].wait_send()
                outward[d, g, i].wait_recv()


def settle(*refs):
    sources, places, held, sem = refs[:4], refs[4:8], refs[8:12], refs[12]
    copies = []
    for src, dst, mid in zip(sources, places, held):
        parts = 2
        size = src.shape[0] // parts
        for part in range(parts):
            at = pl.ds(part * size, size)
            copies.append((pltpu.make_async_copy(src.at[at], mid.at[at], sem.at[0, len(copies)]),
                           pltpu.make_async_copy(mid.at[at], dst.at[at], sem.at[1, len(copies)])))
    for into, _ in copies:
        into.start()
    for into, out in copies:
        into.wait()
        out.start()
    for _, out in copies:
        out.wait()


def on_device(n_seq, n_head, queries, keys, values, out_grad, doc_ids):
    tok, reps, width = queries.shape
    cols = keys.shape[1]
    groups = cols // HD
    rows = tok * reps
    span = (REACH + 1) * tok
    whole = (tok, reps, width) if reps > 1 else (tok, width)
    piece = whole[:-1] + (HD,)
    bf16, f32 = jnp.bfloat16, jnp.float32
    dma = pltpu.SemaphoreType.DMA
    anywhere = pl.BlockSpec(memory_space=pl.ANY)
    vmem = pl.BlockSpec(memory_space=pltpu.VMEM)
    flat = jax.ShapeDtypeStruct(whole, bf16)
    narrow = jax.ShapeDtypeStruct((tok, cols), bf16)
    results = pl.pallas_call(
        functools.partial(kernel, n_seq, n_head, reps),
        out_shape=(flat, flat, narrow, narrow),
        in_specs=[anywhere] * 5,
        out_specs=(anywhere, anywhere, vmem, vmem),
        scratch_shapes=[
            pltpu.VMEM((n_head, groups) + piece, bf16),
            pltpu.VMEM((n_head, groups) + piece, bf16),
            pltpu.VMEM((span, cols), bf16),
            pltpu.VMEM((span, cols), bf16),
            pltpu.VMEM((groups, HD, span), bf16),
            pltpu.VMEM((groups, HD, span), bf16),
            pltpu.VMEM((REACH + 1, 1, tok), jnp.int32),
            pltpu.VMEM((REACH * tok, rows), f32),
            pltpu.VMEM((n_head, groups) + piece, bf16),
            pltpu.VMEM((n_head, groups) + piece, bf16),
            pltpu.VMEM((span, cols), f32),
            pltpu.VMEM((span, cols), f32),
            pltpu.VMEM((REACH, tok, cols), bf16),
            pltpu.VMEM((REACH, tok, cols), bf16),
            pltpu.VMEM((REACH, tok, cols), bf16),
            pltpu.VMEM((REACH, tok, cols), bf16),
            pltpu.VMEM(whole, bf16),
            pltpu.VMEM(whole, bf16),
            dma((REACH, 1 + 2 * groups)), dma((REACH, 1 + 2 * groups)),
            dma((n_head - 1, groups, 2)), dma((n_head - 1, groups, 2)),
            dma((n_head - 1, groups, 2)), dma((n_head - 1, groups, 2)),
            dma((REACH, groups, 2)), dma((REACH, groups, 2)),
            dma((5,)), dma((groups, 2)),
        ],
        compiler_params=pltpu.CompilerParams(
            collective_id=0, has_side_effects=True, vmem_limit_bytes=LIMIT),
        cost_estimate=pl.CostEstimate(
            flops=12 * n_head * groups * rows * span * HD,
            bytes_accessed=8 * rows * width + 8 * tok * cols,
            transcendentals=n_head * groups * rows * REACH * tok),
        name="attention_layer",
    )(queries.reshape(whole), keys, values, out_grad.reshape(whole), doc_ids.reshape(1, tok))
    att, qg, kg, vg = pl.pallas_call(
        settle,
        out_shape=(flat, flat, narrow, narrow),
        in_specs=[anywhere] * 4,
        out_specs=(anywhere,) * 4,
        scratch_shapes=[pltpu.VMEM(x.shape, x.dtype) for x in results] + [dma((2, 8))],
        compiler_params=pltpu.CompilerParams(vmem_limit_bytes=LIMIT),
        name="settle",
    )(*results)
    return (att.reshape(queries.shape), qg.reshape(queries.shape), kg, vg)


def solution(mesh):
    wide, thin = P("seq", "head", None), P("seq", "head")
    return jax.shard_map(
        functools.partial(on_device, mesh.shape["seq"], mesh.shape["head"]),
        mesh=mesh, in_specs=(wide, thin, thin, wide, P("seq")),
        out_specs=(wide, wide, thin, thin), check_vma=False)
```

```python
import functools
import math

import jax
import jax.numpy as jnp
from jax import lax
from jax.experimental import pallas as pl
from jax.experimental.pallas import tpu as pltpu
from jax.sharding import PartitionSpec as P

HD = 128
REACH = 3
LIMIT = 60 * 2**20
MESH = pl.DeviceIdType.MESH


def partner(index, bits):
    out = index
    place = 1
    while place <= bits:
        if bits & place:
            out = out + place * (1 - 2 * ((index // place) % 2))
        place *= 2
    return out


def kernel(
    n_seq, n_head, reps,
    q_ref, k_ref, v_ref, g_ref, doc_ref,
    att_ref, qg_ref, kg_ref, vg_ref,
    qbuf, gbuf, kwin, vwin, kt, vt, docwin, bias, attbuf, qgbuf, kacc, vacc,
    kg_out, vg_out, kg_in, vg_in, qall, gall,
    halo_send, halo_recv, in_send, in_recv, ret_send, ret_recv, grad_send, grad_recv, local_sem, own_sem,
):
    seq, head = lax.axis_index("seq"), lax.axis_index("head")
    tok, cols = k_ref.shape
    rows = tok * reps
    groups = cols // HD
    steps = range(1, REACH + 1)
    peers = range(1, n_head)

    def block(b):
        return pl.ds(b * tok, tok)

    def lanes(g):
        return pl.ds(g * HD, HD)

    def columns(ref, owner, g):
        at = pl.ds(pl.multiple_of(owner * cols + g * HD, HD), HD)
        return ref.at[:, at] if len(ref.shape) == 2 else ref.at[:, :, at]

    def matrix(ref, d, g):
        view = ref.at[d, g]
        return view if len(view.shape) == 2 else view.reshape(rows, HD)

    halo = {}
    for b in steps:
        pairs = [(docwin.at[0], docwin.at[b])]
        for g in range(groups):
            pairs.append((kwin.at[block(0), lanes(g)], kwin.at[block(b), lanes(g)]))
            pairs.append((vwin.at[block(0), lanes(g)], vwin.at[block(b), lanes(g)]))
        for i, (src, dst) in enumerate(pairs):
            halo[b, i] = pltpu.make_async_remote_copy(
                src_ref=src, dst_ref=dst, send_sem=halo_send.at[b - 1, i],
                recv_sem=halo_recv.at[b - 1, i], device_id=(seq + b, head), device_id_type=MESH)
    halos = 1 + 2 * groups
    inward = {}
    outward = {}
    for d in peers:
        other = partner(head, d)
        for g in range(groups):
            for i, (src, dst) in enumerate(((qall, qbuf), (gall, gbuf))):
                inward[d, g, i] = pltpu.make_async_remote_copy(
                    src_ref=columns(src, other, g), dst_ref=dst.at[d, g],
                    send_sem=in_send.at[d - 1, g, i], recv_sem=in_recv.at[d - 1, g, i],
                    device_id=(seq, other), device_id_type=MESH)
            for i, (src, dst) in enumerate(((attbuf, att_ref), (qgbuf, qg_ref))):
                outward[d, g, i] = pltpu.make_async_remote_copy(
                    src_ref=src.at[d, g], dst_ref=columns(dst, head, g),
                    send_sem=ret_send.at[d - 1, g, i], recv_sem=ret_recv.at[d - 1, g, i],
                    device_id=(seq, other), device_id_type=MESH)
    back = {}
    for b in steps:
        for g in range(groups):
            for i, (src, dst) in enumerate(((vg_out, vg_in), (kg_out, kg_in))):
                back[b, g, i] = pltpu.make_async_remote_copy(
                    src_ref=src.at[b - 1, :, lanes(g)], dst_ref=dst.at[b - 1, :, lanes(g)],
                    send_sem=grad_send.at[b - 1, g, i], recv_sem=grad_recv.at[b - 1, g, i],
                    device_id=(seq - b, head), device_id_type=MESH)

    barrier = pltpu.get_barrier_semaphore()
    for d in peers:
        pl.semaphore_signal(barrier, 1, device_id=(seq, partner(head, d)), device_id_type=MESH)
    count = n_head - 1
    for b in steps:
        @pl.when(seq + b < n_seq)
        def _():
            pl.semaphore_signal(barrier, 1, device_id=(seq + b, head), device_id_type=MESH)

        @pl.when(seq >= b)
        def _():
            pl.semaphore_signal(barrier, 1, device_id=(seq - b, head), device_id_type=MESH)
        count = count + jnp.where(seq + b < n_seq, 1, 0) + jnp.where(seq >= b, 1, 0)

    own = [
        pltpu.make_async_copy(src, dst, local_sem.at[i])
        for i, (src, dst) in enumerate((
            (doc_ref, docwin.at[0]), (k_ref, kwin.at[block(0)]), (v_ref, vwin.at[block(0)]),
            (q_ref, qall), (g_ref, gall)))
    ]
    mine = [
        pltpu.make_async_copy(columns(src, head, g), dst.at[0, g], own_sem.at[g, i])
        for g in range(groups) for i, (src, dst) in enumerate(((qall, qbuf), (gall, gbuf)))
    ]
    for copy in own:
        copy.start()
    for copy in own:
        copy.wait()
    for copy in mine:
        copy.start()
    pl.semaphore_wait(barrier, count)

    for d in peers[1:]:
        inward[d, 0, 0].start()
        inward[d, 0, 1].start()
    for g in range(groups):
        for b in reversed(steps):
            @pl.when(seq + b < n_seq)
            def _():
                for i in ((0, 1, 2) if g == 0 else (1 + 2 * g, 2 + 2 * g)):
                    halo[b, i].start()
        for d in (peers if g else peers[:1]):
            inward[d, g, 0].start()
            inward[d, g, 1].start()

    for b in steps:
        @pl.when(seq < b)
        def _():
            kwin[block(b), :] = jnp.zeros((tok, cols), kwin.dtype)
            vwin[block(b), :] = jnp.zeros((tok, cols), vwin.dtype)
            docwin[b] = jnp.full((1, tok), -1, jnp.int32)

    key_of = lax.broadcasted_iota(jnp.int32, (tok, rows), 0)
    token_of = lax.broadcasted_iota(jnp.int32, (tok, rows), 1) // reps
    near = key_of <= token_of
    for copy in mine:
        copy.wait()
    for b in steps:
        @pl.when(seq >= b)
        def _():
            halo[b, 0].wait_recv()

    doc_own = docwin[0].astype(jnp.float32)
    if reps == 1:
        doc_q = doc_own
    else:
        spread = (key_of == token_of).astype(jnp.bfloat16)
        doc_q = jnp.dot(jnp.broadcast_to(doc_own, (16, tok)).astype(jnp.bfloat16), spread,
                        preferred_element_type=jnp.float32)[0:1]

    def same(b):
        doc = jnp.transpose(jnp.broadcast_to(docwin[b].astype(jnp.float32), (tok, tok)))
        return jnp.where(doc[:, 0:1] == doc_q, 0.0, -1e30)

    bias[block(0), :] = jnp.where(near, same(0), same(REACH))
    for b in range(1, REACH):
        bias[block(b), :] = same(b)

    scale = 1.0 / math.sqrt(HD)
    last = REACH * tok

    def folded(x):
        return jnp.concatenate([jnp.where(near, x[:tok], x[last:]), x[tok:last]], axis=0)

    def unfolded(x):
        zero = jnp.zeros((tok, rows), x.dtype)
        return jnp.concatenate(
            [jnp.where(near, x[:tok], zero), x[tok:], jnp.where(near, zero, x[:tok])], axis=0)

    def tile(d, g):
        q = matrix(qbuf, d, g)[...]
        grad = matrix(gbuf, d, g)[...]
        by_last = (((1,), (1,)), ((), ()))
        s = folded(lax.dot_general(kwin[:, lanes(g)], q, by_last, preferred_element_type=jnp.float32))
        s = s + bias[...]
        top = jnp.max(s, axis=0, keepdims=True)
        e = jnp.exp2((s - top) * (scale * math.log2(math.e)))
        p = e * (1.0 / jnp.sum(e, axis=0, keepdims=True))
        dp = folded(lax.dot_general(vwin[:, lanes(g)], grad, by_last, preferred_element_type=jnp.float32))
        delta = jnp.sum(p * dp, axis=0, keepdims=True)
        ds = unfolded(p * (dp - delta) * scale).astype(jnp.bfloat16)
        pb = unfolded(p).astype(jnp.bfloat16)
        att = jnp.dot(vt[g], pb, preferred_element_type=jnp.float32)
        matrix(attbuf, d, g)[...] = jnp.transpose(att).astype(jnp.bfloat16)
        qg = jnp.dot(kt[g], ds, preferred_element_type=jnp.float32)
        matrix(qgbuf, d, g)[...] = jnp.transpose(qg).astype(jnp.bfloat16)
        dv = jnp.dot(pb, grad, preferred_element_type=jnp.float32)
        dk = jnp.dot(ds, q, preferred_element_type=jnp.float32)
        if d == 0:
            vacc[:, lanes(g)] = dv
            kacc[:, lanes(g)] = dk
        else:
            vacc[:, lanes(g)] += dv
            kacc[:, lanes(g)] += dk

    done = [pltpu.make_async_copy(src.at[0, g], columns(dst, head, g), own_sem.at[g, i])
            for g in range(groups) for i, (src, dst) in enumerate(((attbuf, att_ref), (qgbuf, qg_ref)))]
    for g in range(groups):
        for b in steps:
            @pl.when(seq >= b)
            def _():
                halo[b, 1 + 2 * g].wait_recv()
                halo[b, 2 + 2 * g].wait_recv()
        kt[g] = jnp.transpose(kwin[:, lanes(g)])
        vt[g] = jnp.transpose(vwin[:, lanes(g)])
        for d in range(n_head):
            if d:
                inward[d, g, 0].wait_recv()
                inward[d, g, 1].wait_recv()
            tile(d, g)
            if d:
                outward[d, g, 0].start()
                outward[d, g, 1].start()
            else:
                done[2 * g].start()
                done[2 * g + 1].start()
        for b in reversed(steps):
            vg_out[b - 1, :, lanes(g)] = vacc[block(b), lanes(g)].astype(jnp.bfloat16)
            kg_out[b - 1, :, lanes(g)] = kacc[block(b), lanes(g)].astype(jnp.bfloat16)

            @pl.when(seq >= b)
            def _():
                back[b, g, 0].start()
                back[b, g, 1].start()

    for b in steps:
        @pl.when(seq + b < n_seq)
        def _():
            for g in range(groups):
                for i in range(2):
                    back[b, g, i].wait_recv()
            vacc[block(0), :] += vg_in[b - 1].astype(jnp.float32)
            kacc[block(0), :] += kg_in[b - 1].astype(jnp.float32)
    vg_ref[...] = vacc[block(0), :].astype(vg_ref.dtype)
    kg_ref[...] = kacc[block(0), :].astype(kg_ref.dtype)

    for copy in done:
        copy.wait()
    for b in steps:
        @pl.when(seq + b < n_seq)
        def _():
            for i in range(halos):
                halo[b, i].wait_send()

        @pl.when(seq >= b)
        def _():
            for g in range(groups):
                for i in range(2):
                    back[b, g, i].wait_send()
    for d in peers:
        for g in range(groups):
            for i in range(2):
                inward[d, g, i].wait_send()
                outward[d, g, i].wait_send()
                outward[d, g, i].wait_recv()


def settle(*refs):
    sources, places, held, sem = refs[:4], refs[4:8], refs[8:12], refs[12]
    copies = []
    for src, dst, mid in zip(sources, places, held):
        parts = 4 if len(copies) < 8 else 1
        size = src.shape[0] // parts
        for part in range(parts):
            at = pl.ds(part * size, size)
            copies.append((pltpu.make_async_copy(src.at[at], mid.at[at], sem.at[0, len(copies)]),
                           pltpu.make_async_copy(mid.at[at], dst.at[at], sem.at[1, len(copies)])))
    for into, _ in copies:
        into.start()
    for into, out in copies:
        into.wait()
        out.start()
    for _, out in copies:
        out.wait()


def on_device(n_seq, n_head, queries, keys, values, out_grad, doc_ids):
    tok, reps, width = queries.shape
    cols = keys.shape[1]
    groups = cols // HD
    rows = tok * reps
    span = (REACH + 1) * tok
    whole = (tok, reps, width) if reps > 1 else (tok, width)
    piece = whole[:-1] + (HD,)
    bf16, f32 = jnp.bfloat16, jnp.float32
    dma = pltpu.SemaphoreType.DMA
    anywhere = pl.BlockSpec(memory_space=pl.ANY)
    vmem = pl.BlockSpec(memory_space=pltpu.VMEM)
    flat = jax.ShapeDtypeStruct(whole, bf16)
    narrow = jax.ShapeDtypeStruct((tok, cols), bf16)
    results = pl.pallas_call(
        functools.partial(kernel, n_seq, n_head, reps),
        out_shape=(flat, flat, narrow, narrow),
        in_specs=[anywhere] * 5,
        out_specs=(anywhere, anywhere, vmem, vmem),
        scratch_shapes=[
            pltpu.VMEM((n_head, groups) + piece, bf16),
            pltpu.VMEM((n_head, groups) + piece, bf16),
            pltpu.VMEM((span, cols), bf16),
            pltpu.VMEM((span, cols), bf16),
            pltpu.VMEM((groups, HD, span), bf16),
            pltpu.VMEM((groups, HD, span), bf16),
            pltpu.VMEM((REACH + 1, 1, tok), jnp.int32),
            pltpu.VMEM((REACH * tok, rows), f32),
            pltpu.VMEM((n_head, groups) + piece, bf16),
            pltpu.VMEM((n_head, groups) + piece, bf16),
            pltpu.VMEM((span, cols), f32),
            pltpu.VMEM((span, cols), f32),
            pltpu.VMEM((REACH, tok, cols), bf16),
            pltpu.VMEM((REACH, tok, cols), bf16),
            pltpu.VMEM((REACH, tok, cols), bf16),
            pltpu.VMEM((REACH, tok, cols), bf16),
            pltpu.VMEM(whole, bf16),
            pltpu.VMEM(whole, bf16),
            dma((REACH, 1 + 2 * groups)), dma((REACH, 1 + 2 * groups)),
            dma((n_head - 1, groups, 2)), dma((n_head - 1, groups, 2)),
            dma((n_head - 1, groups, 2)), dma((n_head - 1, groups, 2)),
            dma((REACH, groups, 2)), dma((REACH, groups, 2)),
            dma((5,)), dma((groups, 2)),
        ],
        compiler_params=pltpu.CompilerParams(
            collective_id=0, has_side_effects=True, vmem_limit_bytes=LIMIT),
        cost_estimate=pl.CostEstimate(
            flops=12 * n_head * groups * rows * span * HD,
            bytes_accessed=8 * rows * width + 8 * tok * cols,
            transcendentals=n_head * groups * rows * REACH * tok),
        name="attention_layer",
    )(queries.reshape(whole), keys, values, out_grad.reshape(whole), doc_ids.reshape(1, tok))
    att, qg, kg, vg = pl.pallas_call(
        settle,
        out_shape=(flat, flat, narrow, narrow),
        in_specs=[anywhere] * 4,
        out_specs=(anywhere,) * 4,
        scratch_shapes=[pltpu.VMEM(x.shape, x.dtype) for x in results] + [dma((2, 10))],
        compiler_params=pltpu.CompilerParams(vmem_limit_bytes=LIMIT),
        name="settle",
    )(*results)
    return (att.reshape(queries.shape), qg.reshape(queries.shape), kg, vg)


def solution(mesh):
    wide, thin = P("seq", "head", None), P("seq", "head")
    return jax.shard_map(
        functools.partial(on_device, mesh.shape["seq"], mesh.shape["head"]),
        mesh=mesh, in_specs=(wide, thin, thin, wide, P("seq")),
        out_specs=(wide, wide, thin, thin), check_vma=False)
```
